512 devices in a mesh: span: 32 (over z, x), sub: 16 (over y, core).
Axes of the slice: x: 4, y: 8, z: 8, core: 2. Of those that a mesh axis runs over, the one named last changes fastest.
Arguments:
- stress: bfloat16 [512, 768, 128], P(('span', 'sub')), may hold values from -6 to 6
- history: float32 [8, 512, 768], P(None, ('span', 'sub')), may hold values from -6 to 6
- retard: float32 [8], replicated, may hold values from 0.3 to 30
- compliance: float32 [8], replicated, may hold values from 0.2 to 2
- micro: float32 [512, 768], P(('span', 'sub')), may hold values from 0.5 to 5
- lengths: int32 [512], P(('span', 'sub')), may hold values from 1 to 768, 131072 in all
- multiplier_index: int32 [512, 768], P(('span', 'sub')), may hold values from 0 to 131071, as said below
- dual_block: bfloat16 [512, 768, 768], P(('span', 'sub')), may hold values from -1 to 4, as said below
- corner_map: bfloat16 [512, 768, 128], P(('span', 'sub')), may hold values from -0.21875 to 0.21875
- coarse_stiffness_inverse: float32 [32, 128, 128], P('span'), may hold values from -1 to 4, as said below
Outputs:
- solution: float32 [131072, 128], P(('span', 'sub'))
- residual: float32 [131072, 128], P(('span', 'sub'))
The draws below stay inside these ranges and needn't reach their ends.
Inputs may be any that keep to these rules, and one draw needn't show every extreme that they name: `multiplier_index`: each slot of a subdomain names a multiplier held by its own device or by the device of the same sub index in one of the two neighbouring spans; multipliers 0 and 131071 are named in every draw. `dual_block`: each block is symmetric with a diagonal between 1 and 4. `coarse_stiffness_inverse`: each span's matrix is symmetric with a diagonal between 1 and 4.
All inputs are finite; a program needn't handle non-finite values. No bound on the sum of `lengths` on one device may be relied on, other than what follows from the above.
Results may differ from the reference program's by a relative error of at most 0.024.
Values may be sent and summed in bfloat16 or wider, within the bound.
A program may use at most 64 MiB of HBM per device.

```python
import math
import jax
import jax.numpy as jnp
import numpy as np
from jax import lax

MULTIPLIER_SLOTS = 768
C = 128
KEL = 8
ITERS = 2
SUB_DEV = 1
LOAD_CASES = 128
LAM_DEV = 256
SUBDOMAIN_TOTAL = 512
NLAM = 131072
SPANS = 32
N_SPAN = 32
N_SUB = 16
DEVICES = 512


def draw_multiplier_index(key, part):
    first_key = jax.random.fold_in(key, 11)
    second_key = jax.random.fold_in(key, 12)
    device = (jnp.arange(SUBDOMAIN_TOTAL) // SUB_DEV)[:, None]
    span_of = device // N_SUB
    side = device % N_SUB
    offset = jax.random.randint(first_key, (SUBDOMAIN_TOTAL, MULTIPLIER_SLOTS), -1, 2)
    owner_span = jnp.clip(span_of + offset, 0, N_SPAN - 1)
    row_pick = jax.random.randint(second_key, (SUBDOMAIN_TOTAL, MULTIPLIER_SLOTS), 0, LAM_DEV)
    result = (owner_span * N_SUB + side) * LAM_DEV + row_pick
    result = result.at[0, 0].set(0)
    result = result.at[SUBDOMAIN_TOTAL - 1, 0].set(NLAM - 1)
    return result.astype(jnp.int32)


def draw_dual_block(key, part):
    first_key = jax.random.fold_in(key, 21)
    second_key = jax.random.fold_in(key, 22)
    bound_off = 0.5 / MULTIPLIER_SLOTS ** 0.5
    raw = jax.random.uniform(first_key, (SUBDOMAIN_TOTAL, MULTIPLIER_SLOTS, MULTIPLIER_SLOTS), jnp.float32, -bound_off, bound_off)
    sym = 0.5 * (raw + jnp.swapaxes(raw, 1, 2))
    diag_vals = jax.random.uniform(second_key, (SUBDOMAIN_TOTAL, MULTIPLIER_SLOTS), jnp.float32, 1.0, 2.0)
    eye_mask = jnp.eye(MULTIPLIER_SLOTS, dtype=jnp.float32)[None]
    return (sym * (1.0 - eye_mask) + eye_mask * diag_vals[:, :, None]).astype(jnp.bfloat16)


def draw_coarse_stiffness_inverse(key, part):
    first_key = jax.random.fold_in(key, 31)
    second_key = jax.random.fold_in(key, 32)
    bound_off = 0.5 / C ** 0.5
    raw = jax.random.uniform(first_key, (SPANS, C, C), jnp.float32, -bound_off, bound_off)
    sym = 0.5 * (raw + jnp.swapaxes(raw, 1, 2))
    diag_vals = jax.random.uniform(second_key, (SPANS, C), jnp.float32, 1.0, 2.0)
    eye_mask = jnp.eye(C, dtype=jnp.float32)[None]
    return sym * (1.0 - eye_mask) + eye_mask * diag_vals[:, :, None]


def levels(stream_key, extent, cuts, least, top_value):
    level = 1.0
    for axis_at, shards_of in cuts:
        draws = jax.random.uniform(jax.random.fold_in(jax.random.fold_in(stream_key, 6), axis_at), (shards_of,), jnp.float32, least / len(cuts), top_value / len(cuts))
        level = level * jnp.repeat(jnp.exp(draws), extent[axis_at] // shards_of).reshape((-1,) + (1,) * (len(extent) - 1 - axis_at))
    return level


def split_up(number_of, total, bound, skew):
    weights = [(1 << 20) // math.isqrt(rank ** skew) + 1 for rank in range(2, number_of + 1)]
    spare, holding = total - bound - (number_of - 1), [1] * (number_of - 1)
    while spare > 0:
        movable = [i for i in range(number_of - 1) if holding[i] < bound]
        whole, remaining = sum([weights[i] for i in movable]), spare
        for i in movable:
            extra = min(bound - holding[i], max(1, remaining * weights[i] // whole), spare)
            holding[i] = holding[i] + extra
            spare = spare - extra
    return np.array([bound] + holding)


def uneven(key, number_of, total, reach, lean):
    if number_of == 2:
        one = jax.random.randint(key, (), max(1, total - reach), min(reach, total - 1) + 1)
        return jnp.stack([one, total - one])
    sizes = jnp.asarray(split_up(number_of, total, reach, lean), jnp.int32)
    pairs = (number_of - 1) // 2
    source_of, receiver = sizes[1:1 + 2 * pairs:2], sizes[2:2 + 2 * pairs:2]
    margin = jnp.minimum(source_of - 1, reach - receiver)
    passed = jax.random.randint(jax.random.fold_in(key, 1), (pairs,), 0, 1 << 20) % (margin + 1)
    sizes = sizes.at[1:1 + 2 * pairs:2].set(source_of - passed).at[2:2 + 2 * pairs:2].set(receiver + passed)
    return sizes[jax.random.permutation(jax.random.fold_in(key, 2), number_of)]


def bell_draw(own_key, dims, deviation, most, split=(), kind=jnp.bfloat16):
    factor_of = levels(own_key, dims, split, -0.22, 0.18) if split else 1.0
    values = jax.random.normal(own_key, dims, jnp.float32) * deviation * factor_of
    return jnp.minimum(jnp.maximum(values, -most), most).astype(kind)


def setup_inputs(seed: int = 0) -> dict:
    splits = jax.random.split(jax.random.key(seed), 11)
    stress = bell_draw(splits[0], (SUBDOMAIN_TOTAL, MULTIPLIER_SLOTS, LOAD_CASES), 1.0, 6.0, ((0, 512),))
    history = bell_draw(splits[1], (KEL, SUBDOMAIN_TOTAL, MULTIPLIER_SLOTS), 1.0, 6.0, ((1, 512),), jnp.float32)
    retard = jnp.clip(jnp.exp(jax.random.uniform(splits[2], (KEL,), jnp.float32, math.log(0.3), math.log(30.0))), 0.3, 30.0)
    compliance = jnp.clip(jnp.exp(jax.random.uniform(splits[3], (KEL,), jnp.float32, math.log(0.2), math.log(2.0))), 0.2, 2.0)
    micro = jnp.clip(jnp.exp(math.log(5.0) - 2.3025851 * jax.random.uniform(splits[4], (SUBDOMAIN_TOTAL, MULTIPLIER_SLOTS), jnp.float32) ** levels(splits[4], (SUBDOMAIN_TOTAL, MULTIPLIER_SLOTS), ((0, 512),), -0.2, 0.2)), 0.5, 5.0)
    lengths = uneven(splits[5], SUBDOMAIN_TOTAL, SUBDOMAIN_TOTAL * MULTIPLIER_SLOTS // 3, MULTIPLIER_SLOTS, 2).astype(jnp.int32)
    multiplier_index = draw_multiplier_index(jax.random.fold_in(splits[10], 71), 0)
    dual_block = draw_dual_block(jax.random.fold_in(splits[10], 71), 0)
    corner_map = bell_draw(splits[8], (SUBDOMAIN_TOTAL, MULTIPLIER_SLOTS, C), MULTIPLIER_SLOTS ** -0.5, 0.21875, ((0, 512),))
    coarse_stiffness_inverse = draw_coarse_stiffness_inverse(jax.random.fold_in(splits[10], 71), 0)
    return {"stress": stress, "history": history, "retard": retard, "compliance": compliance, "micro": micro, "lengths": lengths, "multiplier_index": multiplier_index, "dual_block": dual_block, "corner_map": corner_map, "coarse_stiffness_inverse": coarse_stiffness_inverse}


def reference(stress, history, retard, compliance, micro, lengths, multiplier_index, dual_block, corner_map, coarse_stiffness_inverse):
    live = (jnp.arange(MULTIPLIER_SLOTS)[None, :] < lengths[:, None]).astype(jnp.float32)
    weight_k = 1.0 - jnp.exp(-1.0 / retard)
    creep = jnp.sum(weight_k * compliance)
    past = jnp.sum(weight_k[:, None, None] * history, axis=0)
    relaxed = micro / (1.0 + micro)
    signal = stress.astype(jnp.float32)
    load = ((creep + 0.5 * relaxed[:, :, None]) * signal - past[:, :, None]) * live[:, :, None]
    flat_index = multiplier_index.reshape(-1)

    def assemble(local):
        return jnp.zeros((NLAM, LOAD_CASES), jnp.float32).at[flat_index].add(local.reshape(-1, LOAD_CASES))

    per_span = SUBDOMAIN_TOTAL // N_SPAN

    def apply_operator(direction):
        gathered = (direction[multiplier_index] * live[:, :, None]).astype(jnp.bfloat16)
        blocks = dual_block.reshape(DEVICES, SUB_DEV, MULTIPLIER_SLOTS, MULTIPLIER_SLOTS)
        values = gathered.reshape(DEVICES, SUB_DEV, MULTIPLIER_SLOTS, LOAD_CASES)

        def one_device(pair):
            return jnp.einsum("smn,snr->smr", pair[0].astype(jnp.float32), pair[1].astype(jnp.float32))

        local = lax.map(one_device, (blocks, values)).reshape(SUBDOMAIN_TOTAL, MULTIPLIER_SLOTS, LOAD_CASES)
        slot_mappings = corner_map.astype(jnp.float32).reshape(N_SPAN, per_span, MULTIPLIER_SLOTS, C)
        span_entries = gathered.astype(jnp.float32).reshape(N_SPAN, per_span, MULTIPLIER_SLOTS, LOAD_CASES)
        corner_residual = jnp.einsum("dyzu,dyzl->dul", slot_mappings, span_entries)
        corner_update = jnp.einsum("mtg,mgf->mtf", coarse_stiffness_inverse, corner_residual, precision=lax.Precision.HIGHEST).astype(jnp.bfloat16)
        spread_corners = jnp.einsum("ygtf,yfw->ygtw", slot_mappings, corner_update.astype(jnp.float32)).reshape(SUBDOMAIN_TOTAL, MULTIPLIER_SLOTS, LOAD_CASES)
        return assemble((local + spread_corners) * live[:, :, None])

    rhs = assemble(load)
    solution = jnp.zeros((NLAM, LOAD_CASES), jnp.float32)
    residual = rhs
    direction = rhs
    norm_now = jnp.sum(residual * residual, axis=0)
    for step in range(ITERS):
        image = apply_operator(direction)
        alpha = norm_now / jnp.sum(direction * image, axis=0)
        solution = solution + alpha * direction
        residual = residual - alpha * image
        norm_next = jnp.sum(residual * residual, axis=0)
        direction = residual + (norm_next / norm_now) * direction
        norm_now = norm_next
    return solution, residual
```

```python
import functools

import jax
import jax.numpy as jnp
from jax import lax
from jax.experimental import pallas as pl
from jax.experimental.pallas import tpu as pltpu
from jax.sharding import PartitionSpec as P

MESH = pl.DeviceIdType.MESH
F32 = jnp.float32
BF16 = jnp.bfloat16
CONTRIB = jnp.bfloat16
OWN = 256
SLOTS = 768
CASES = 128
CORNERS = 128
HALF = CORNERS // 2
SUMS = 16
ROWS = 64


def dot(a, b):
    return jnp.dot(a, b, preferred_element_type=F32)


def two_parts(x):
    high = x.astype(BF16)
    return high, (x - high.astype(F32)).astype(BF16)


def column_sum(x):
    return jnp.sum(x, axis=0, keepdims=True)


def as_column(row):
    return jnp.transpose(jnp.broadcast_to(row, (CASES, SLOTS)))


def sum_rows(first, second):
    row = lax.broadcasted_iota(jnp.int32, (SUMS, CASES), 0)
    out = jnp.zeros((SUMS, CASES), F32)
    for base, value in ((0, first), (3, second)):
        rest = value
        for i in range(3):
            part = rest.astype(BF16).astype(F32)
            rest = rest - part
            out = jnp.where(row == base + i, part, out)
    return out


def kernel(
    spans,
    subs,
    retard,
    compliance,
    lengths,
    stress_hbm,
    history_hbm,
    micro_hbm,
    index_hbm,
    dual_hbm,
    corner_hbm,
    stiff_hbm,
    solution_ref,
    residual_ref,
    stress,
    history,
    micro,
    index,
    dual,
    corner,
    stiff,
    pick,
    pick_t,
    corner_t,
    corner_w,
    split,
    window,
    local_window,
    v,
    contrib_out,
    contrib_in,
    w_part,
    w_full,
    chip_in,
    ring_out,
    ring_in,
    pair_out,
    pair_in,
    totals,
    load_sem,
    contrib_send,
    contrib_recv,
    halo_send,
    halo_recv,
    chip_sem,
    ring_send,
    ring_recv,
    pair_sem,
    total_send,
    total_recv,
):
    p = lax.axis_index("span")
    s = lax.axis_index("sub")
    chips = subs // 2
    core = lax.rem(s, 2)
    partner = (p, s + 1 - 2 * core)
    before = (lax.rem(p + spans - 1, spans), s)
    after = (lax.rem(p + 1, spans), s)
    mine = pl.ds(pl.multiple_of(core * HALF, HALF), HALF)
    theirs = pl.ds(pl.multiple_of((1 - core) * HALF, HALF), HALF)

    loads = [
        pltpu.make_async_copy(src, dst, load_sem.at[i])
        for i, (src, dst) in enumerate(
            (
                (index_hbm, index),
                (micro_hbm, micro),
                (history_hbm, history),
                (stress_hbm.at[0], stress),
                (corner_hbm.at[0], corner),
                (dual_hbm.at[0], dual),
                (stiff_hbm.at[0], stiff),
            )
        )
    ]
    for copy in loads:
        copy.start()

    barrier = pltpu.get_barrier_semaphore()

    def greet_span(d, carry):
        pl.semaphore_signal(
            barrier, inc=1, device_id=(lax.rem(p + d, spans), s), device_id_type=MESH
        )
        return carry

    def greet_chip(d, carry):
        pl.semaphore_signal(
            barrier, inc=1, device_id=(p, lax.rem(s + 2 * d, subs)), device_id_type=MESH
        )
        return carry

    lax.fori_loop(1, spans, greet_span, 0)
    lax.fori_loop(1, chips, greet_chip, 0)
    pl.semaphore_signal(barrier, inc=1, device_id=partner, device_id_type=MESH)

    loads[0].wait()
    slot = lax.broadcasted_iota(jnp.int32, (1, SLOTS), 1)
    owner_span = index[...] // (OWN * subs)
    place = (owner_span - p + 1) * OWN + lax.rem(index[...], OWN)
    place = jnp.where(slot < lengths[0], place, -1)

    def build_pick(i, carry):
        rows = pl.ds(pl.multiple_of(i * ROWS, ROWS), ROWS)
        at = lax.broadcasted_iota(jnp.int32, (ROWS, SLOTS), 0) + i * ROWS
        pick[rows, :] = jnp.where(at == place, 1.0, 0.0).astype(BF16)
        return carry

    lax.fori_loop(0, SLOTS // ROWS, build_pick, 0)

    loads[1].wait()
    loads[2].wait()
    creep = jnp.zeros((1, SLOTS), F32)
    past = jnp.zeros((1, SLOTS), F32)
    for k in range(history.shape[0]):
        weight = 1.0 - jnp.exp(-1.0 / jnp.full((1, SLOTS), retard[k], F32))
        creep = creep + weight * compliance[k]
        past = past + weight * history[k]
    relaxed = micro[...] / (1.0 + micro[...])
    scale = as_column(creep + 0.5 * relaxed)
    past = as_column(past)
    loads[3].wait()
    load = scale * stress[...].astype(F32) - past
    high, low = two_parts(load)
    split[:, :CASES] = high
    split[:, CASES:] = low

    def picked(rows):
        both = dot(pick[rows, :], split[...])
        return both[:, :CASES] + both[:, CASES:]

    def contrib_copies(k):
        return [
            pltpu.make_async_remote_copy(
                src_ref=contrib_out.at[k, i],
                dst_ref=contrib_in.at[k, i],
                send_sem=contrib_send.at[k, i],
                recv_sem=contrib_recv.at[k, i],
                device_id=to,
                device_id_type=MESH,
            )
            for i, to in enumerate((before, after))
        ]

    def halo_copies(k):
        return [
            pltpu.make_async_remote_copy(
                src_ref=window.at[k, pl.ds(OWN, OWN)],
                dst_ref=window.at[k, pl.ds(2 * OWN if i == 0 else 0, OWN)],
                send_sem=halo_send.at[k, i],
                recv_sem=halo_recv.at[k, i],
                device_id=to,
                device_id_type=MESH,
            )
            for i, to in enumerate((before, after))
        ]

    def chip_copy(k):
        return pltpu.make_async_remote_copy(
            src_ref=w_part.at[k, theirs],
            dst_ref=chip_in.at[k],
            send_sem=chip_sem.at[k, 0],
            recv_sem=chip_sem.at[k, 1],
            device_id=partner,
            device_id_type=MESH,
        )

    def ring_copies(k):
        return [
            pltpu.make_async_remote_copy(
                src_ref=ring_out.at[k],
                dst_ref=ring_in.at[k, d - 1],
                send_sem=ring_send.at[k, d - 1],
                recv_sem=ring_recv.at[k, d - 1],
                device_id=(p, lax.rem(s + 2 * d, subs)),
                device_id_type=MESH,
            )
            for d in range(1, chips)
        ]

    def pair_copy(k):
        return pltpu.make_async_remote_copy(
            src_ref=pair_out.at[k],
            dst_ref=pair_in.at[k],
            send_sem=pair_sem.at[k, 0],
            recv_sem=pair_sem.at[k, 1],
            device_id=partner,
            device_id_type=MESH,
        )

    def total_copy(k, d):
        return pltpu.make_async_remote_copy(
            src_ref=totals.at[k, 0],
            dst_ref=totals.at[k, d],
            send_sem=total_send.at[k, d],
            recv_sem=total_recv.at[k, d],
            device_id=(lax.rem(p + d, spans), s),
            device_id_type=MESH,
        )

    def each_total(k, act):
        def step(d, carry):
            act(total_copy(k, d))
            return carry

        lax.fori_loop(1, spans, step, 0)

    previous, own, following = (slice(i * OWN, (i + 1) * OWN) for i in range(3))

    def assembled(k, own_part):
        for copy in contrib_copies(k):
            copy.wait_recv()
        return own_part + contrib_in[k, 0].astype(F32) + contrib_in[k, 1].astype(F32)

    contrib_out[0, 0] = picked(previous).astype(CONTRIB)
    contrib_out[0, 1] = picked(following).astype(CONTRIB)
    pl.semaphore_wait(barrier, spans + chips - 1)
    for copy in contrib_copies(0):
        copy.start()
    own_part = picked(own)

    place_t = as_column(place.astype(F32))

    def build_pick_t(j, carry):
        lanes = pl.ds(pl.multiple_of(j * CASES, CASES), CASES)
        at = lax.broadcasted_iota(jnp.int32, (SLOTS, CASES), 1) + j * CASES
        pick_t[:, lanes] = jnp.where(place_t == at.astype(F32), 1.0, 0.0).astype(BF16)
        return carry

    lax.fori_loop(0, SLOTS // CASES, build_pick_t, 0)
    loads[4].wait()
    corner_t[...] = jnp.transpose(corner[...].astype(F32)).astype(BF16)
    high, low = two_parts(dot(pick[...], corner[...]))
    corner_w[:, :CORNERS] = high
    corner_w[:, CORNERS:] = low
    loads[5].wait()
    loads[6].wait()

    v[0] = assembled(0, own_part)
    for k in range(2):
        window[k, own] = v[k].astype(BF16)
        for copy in halo_copies(k):
            copy.start()
        norm = column_sum(v[k] * v[k])
        for copy in halo_copies(k):
            copy.wait_recv()
        u = dot(pick_t[...], window[k]).astype(BF16)
        w_part[k] = dot(corner_t[...], u)
        chip_copy(k).start()
        y = dot(dual[...], u)
        ring_sums = sum_rows(norm, column_sum(u.astype(F32) * y))
        chip_copy(k).wait_recv()
        half = w_part[k, mine] + chip_in[k]
        ring_out[k, :HALF] = half.astype(BF16)
        ring_out[k, HALF:] = ring_sums.astype(BF16)
        for copy in ring_copies(k):
            copy.start()
        high, low = two_parts(y)
        split[:, :CASES] = high
        split[:, CASES:] = low
        for block in (previous, own, following):
            local_window[block, :] = picked(block)
        for d, copy in enumerate(ring_copies(k)):
            copy.wait_recv()
        for d in range(chips - 1):
            half = half + ring_in[k, d, :HALF].astype(F32)
            ring_sums = ring_sums + ring_in[k, d, HALF:].astype(F32)
        pair_out[k, :HALF] = half
        pair_out[k, HALF:] = ring_sums
        pair_copy(k).start()
        w_full[mine, :] = half
        pair_copy(k).wait_recv()
        w_full[theirs, :] = pair_in[k, :HALF]
        ring_sums = ring_sums + pair_in[k, HALF:]
        w = w_full[...]
        z = jnp.dot(stiff[...], w, precision=lax.Precision.HIGHEST, preferred_element_type=F32)
        z_narrow = z.astype(BF16)
        z_twice = jnp.concatenate([z_narrow, z_narrow], axis=0)

        def image(rows):
            return local_window[rows, :] + dot(corner_w[rows, :], z_twice)

        contrib_out[k + 1, 0] = image(previous).astype(CONTRIB)
        contrib_out[k + 1, 1] = image(following).astype(CONTRIB)
        for copy in contrib_copies(k + 1):
            copy.start()
        coarse = column_sum(w * z_narrow.astype(F32))
        totals[k, 0] = jnp.concatenate(
            [column_sum(ring_sums[0:3]), column_sum(ring_sums[3:6]) + coarse], axis=0
        )
        each_total(k, lambda copy: copy.start())
        own_part = image(own)
        v[k + 1] = assembled(k + 1, own_part)

    for k in range(2):
        each_total(k, lambda copy: copy.wait_recv())
    first = jnp.sum(totals[0], axis=0)
    second = jnp.sum(totals[1], axis=0)
    g00, g01 = first[0:1], first[1:2]
    g11, g12 = second[0:1], second[1:2]
    alpha0 = g00 / g01
    norm1 = g00 - 2.0 * alpha0 * g01 + alpha0 * alpha0 * g11
    beta = norm1 / g00
    grown = 1.0 + beta
    curve = grown * grown * g01 - 2.0 * grown * alpha0 * g11 + alpha0 * alpha0 * g12
    alpha1 = norm1 / curve
    v0, v1, v2 = v[0], v[1], v[2]
    residual1 = v0 - alpha0 * v1
    direction1 = residual1 + beta * v0
    solution_ref[...] = alpha0 * v0 + alpha1 * direction1
    residual_ref[...] = residual1 - alpha1 * (grown * v1 - alpha0 * v2)

    for k in range(3):
        for copy in contrib_copies(k):
            copy.wait_send()
    for k in range(2):
        for copy in halo_copies(k) + [chip_copy(k), pair_copy(k)] + ring_copies(k):
            copy.wait_send()
        each_total(k, lambda copy: copy.wait_send())


def solution(mesh):
    spans, subs = mesh.shape["span"], mesh.shape["sub"]
    chips = subs // 2
    vmem = pl.BlockSpec(memory_space=pltpu.VMEM)
    smem = pl.BlockSpec(memory_space=pltpu.SMEM)
    hbm = pl.BlockSpec(memory_space=pl.ANY)
    dma = pltpu.SemaphoreType.DMA

    def on_device(
        stress,
        history,
        retard,
        compliance,
        micro,
        lengths,
        multiplier_index,
        dual_block,
        corner_map,
        coarse_stiffness_inverse,
    ):
        units = history.shape[0]
        return pl.pallas_call(
            functools.partial(kernel, spans, subs),
            name="creep_step",
            out_shape=[jax.ShapeDtypeStruct((OWN, CASES), F32)] * 2,
            in_specs=[smem] * 3 + [hbm] * 7,
            out_specs=[vmem] * 2,
            scratch_shapes=[
                pltpu.VMEM((SLOTS, CASES), BF16),
                pltpu.VMEM((units, 1, SLOTS), F32),
                pltpu.VMEM((1, SLOTS), F32),
                pltpu.VMEM((1, SLOTS), jnp.int32),
                pltpu.VMEM((SLOTS, SLOTS), BF16),
                pltpu.VMEM((SLOTS, CORNERS), BF16),
                pltpu.VMEM((CORNERS, CORNERS), F32),
                pltpu.VMEM((SLOTS, SLOTS), BF16),
                pltpu.VMEM((SLOTS, SLOTS), BF16),
                pltpu.VMEM((CORNERS, SLOTS), BF16),
                pltpu.VMEM((SLOTS, 2 * CORNERS), BF16),
                pltpu.VMEM((SLOTS, 2 * CASES), BF16),
                pltpu.VMEM((2, SLOTS, CASES), BF16),
                pltpu.VMEM((SLOTS, CASES), F32),
                pltpu.VMEM((3, OWN, CASES), F32),
                pltpu.VMEM((3, 2, OWN, CASES), CONTRIB),
                pltpu.VMEM((3, 2, OWN, CASES), CONTRIB),
                pltpu.VMEM((2, CORNERS, CASES), F32),
                pltpu.VMEM((CORNERS, CASES), F32),
                pltpu.VMEM((2, HALF, CASES), F32),
                pltpu.VMEM((2, HALF + SUMS, CASES), BF16),
                pltpu.VMEM((2, chips - 1, HALF + SUMS, CASES), BF16),
                pltpu.VMEM((2, HALF + SUMS, CASES), F32),
                pltpu.VMEM((2, HALF + SUMS, CASES), F32),
                pltpu.VMEM((2, spans, 2, CASES), F32),
                dma((7,)),
                dma((3, 2)),
                dma((3, 2)),
                dma((2, 2)),
                dma((2, 2)),
                dma((2, 2)),
                dma((2, chips - 1)),
                dma((2, chips - 1)),
                dma((2, 2)),
                dma((2, spans)),
                dma((2, spans)),
            ],
            compiler_params=pltpu.CompilerParams(
                collective_id=0, has_side_effects=True, vmem_limit_bytes=32 * 2**20
            ),
        )(
            retard,
            compliance,
            lengths,
            stress,
            history,
            micro,
            multiplier_index,
            dual_block,
            corner_map,
            coarse_stiffness_inverse,
        )

    rows = P(("span", "sub"), None)
    blocks = P(("span", "sub"), None, None)
    return jax.shard_map(
        on_device,
        mesh=mesh,
        in_specs=(
            blocks,
            P(None, ("span", "sub"), None),
            P(),
            P(),
            rows,
            P(("span", "sub")),
            rows,
            blocks,
            blocks,
            P("span", None, None),
        ),
        out_specs=(rows, rows),
        check_vma=False,
    )
```

```python
import functools

import jax
import jax.numpy as jnp
from jax import lax
from jax.experimental import pallas as pl
from jax.experimental.pallas import tpu as pltpu
from jax.sharding import PartitionSpec as P

MESH = pl.DeviceIdType.MESH
F32 = jnp.float32
BF16 = jnp.bfloat16
CONTRIB = jnp.bfloat16
OWN = 256
SLOTS = 768
CASES = 128
CORNERS = 128
HALF = CORNERS // 2
SUMS = 16
ROWS = 64


def dot(a, b):
    return jnp.dot(a, b, preferred_element_type=F32)


def two_parts(x):
    high = x.astype(BF16)
    return high, (x - high.astype(F32)).astype(BF16)


def column_sum(x):
    return jnp.sum(x, axis=0, keepdims=True)


def as_column(row):
    return jnp.transpose(jnp.broadcast_to(row, (CASES, SLOTS)))


def sum_rows(first, second):
    row = lax.broadcasted_iota(jnp.int32, (SUMS, CASES), 0)
    out = jnp.zeros((SUMS, CASES), F32)
    for base, value in ((0, first), (3, second)):
        rest = value
        for i in range(3):
            part = rest.astype(BF16).astype(F32)
            rest = rest - part
            out = jnp.where(row == base + i, part, out)
    return out


def kernel(
    spans,
    subs,
    retard,
    compliance,
    lengths,
    stress_hbm,
    history_hbm,
    micro_hbm,
    index_hbm,
    dual_hbm,
    corner_hbm,
    stiff_hbm,
    solution_ref,
    residual_ref,
    stress,
    history,
    micro,
    index,
    dual,
    corner,
    stiff,
    pick,
    pick_t,
    corner_t,
    corner_w,
    split,
    window,
    local_window,
    v,
    contrib_out,
    contrib_in,
    w_part,
    w_full,
    chip_in,
    ring_out,
    ring_in,
    pair_out,
    pair_in,
    totals,
    load_sem,
    contrib_send,
    contrib_recv,
    chip_sem,
    ring_send,
    ring_recv,
    pair_sem,
    total_send,
    total_recv,
):
    p = lax.axis_index("span")
    s = lax.axis_index("sub")
    chips = subs // 2
    core = lax.rem(s, 2)
    partner = (p, s + 1 - 2 * core)
    mine = pl.ds(pl.multiple_of(core * HALF, HALF), HALF)
    theirs = pl.ds(pl.multiple_of((1 - core) * HALF, HALF), HALF)

    loads = [
        pltpu.make_async_copy(src, dst, load_sem.at[i])
        for i, (src, dst) in enumerate(
            (
                (index_hbm, index),
                (micro_hbm, micro),
                (history_hbm, history),
                (stress_hbm.at[0], stress),
                (corner_hbm.at[0], corner),
                (dual_hbm.at[0], dual),
                (stiff_hbm.at[0], stiff),
            )
        )
    ]
    for copy in loads:
        copy.start()

    barrier = pltpu.get_barrier_semaphore()

    def greet_span(d, carry):
        pl.semaphore_signal(
            barrier, inc=1, device_id=(lax.rem(p + d, spans), s), device_id_type=MESH
        )
        return carry

    def greet_chip(d, carry):
        pl.semaphore_signal(
            barrier, inc=1, device_id=(p, lax.rem(s + 2 * d, subs)), device_id_type=MESH
        )
        return carry

    lax.fori_loop(1, spans, greet_span, 0)
    lax.fori_loop(1, chips, greet_chip, 0)
    pl.semaphore_signal(barrier, inc=1, device_id=partner, device_id_type=MESH)

    loads[0].wait()
    slot = lax.broadcasted_iota(jnp.int32, (1, SLOTS), 1)
    owner_span = index[...] // (OWN * subs)
    place = (owner_span - p + 1) * OWN + lax.rem(index[...], OWN)
    place = jnp.where(slot < lengths[0], place, -1)

    def build_pick(i, carry):
        rows = pl.ds(pl.multiple_of(i * ROWS, ROWS), ROWS)
        at = lax.broadcasted_iota(jnp.int32, (ROWS, SLOTS), 0) + i * ROWS
        pick[rows, :] = jnp.where(at == place, 1.0, 0.0).astype(BF16)
        return carry

    lax.fori_loop(0, SLOTS // ROWS, build_pick, 0)

    loads[1].wait()
    loads[2].wait()
    creep = jnp.zeros((1, SLOTS), F32)
    past = jnp.zeros((1, SLOTS), F32)
    for k in range(history.shape[0]):
        weight = 1.0 - jnp.exp(-1.0 / jnp.full((1, SLOTS), retard[k], F32))
        creep = creep + weight * compliance[k]
        past = past + weight * history[k]
    relaxed = micro[...] / (1.0 + micro[...])
    scale = as_column(creep + 0.5 * relaxed)
    past = as_column(past)
    loads[3].wait()
    load = scale * stress[...].astype(F32) - past
    high, low = two_parts(load)
    split[:, :CASES] = high
    split[:, CASES:] = low

    def picked(rows):
        both = dot(pick[rows, :], split[...])
        return both[:, :CASES] + both[:, CASES:]

    routes = ((1, 1), (2, 2), (2, 1), (0, -1), (1, -1), (0, -2))

    def contrib_copy(k, i):
        block, onward = routes[i]
        return pltpu.make_async_remote_copy(
            src_ref=contrib_out.at[k, block],
            dst_ref=contrib_in.at[k, i],
            send_sem=contrib_send.at[k, i],
            recv_sem=contrib_recv.at[k, i],
            device_id=(lax.rem(p + spans + onward, spans), s),
            device_id_type=MESH,
        )

    def used_routes(k):
        return range(6) if k < 2 else (2, 3)

    def chip_copy(k):
        return pltpu.make_async_remote_copy(
            src_ref=w_part.at[k, theirs],
            dst_ref=chip_in.at[k],
            send_sem=chip_sem.at[k, 0],
            recv_sem=chip_sem.at[k, 1],
            device_id=partner,
            device_id_type=MESH,
        )

    def ring_copies(k):
        return [
            pltpu.make_async_remote_copy(
                src_ref=ring_out.at[k],
                dst_ref=ring_in.at[k, d - 1],
                send_sem=ring_send.at[k, d - 1],
                recv_sem=ring_recv.at[k, d - 1],
                device_id=(p, lax.rem(s + 2 * d, subs)),
                device_id_type=MESH,
            )
            for d in range(1, chips)
        ]

    def pair_copy(k):
        return pltpu.make_async_remote_copy(
            src_ref=pair_out.at[k],
            dst_ref=pair_in.at[k],
            send_sem=pair_sem.at[k, 0],
            recv_sem=pair_sem.at[k, 1],
            device_id=partner,
            device_id_type=MESH,
        )

    def total_copy(k, d):
        return pltpu.make_async_remote_copy(
            src_ref=totals.at[k, 0],
            dst_ref=totals.at[k, d],
            send_sem=total_send.at[k, d],
            recv_sem=total_recv.at[k, d],
            device_id=(lax.rem(p + d, spans), s),
            device_id_type=MESH,
        )

    def each_total(k, act):
        def step(d, carry):
            act(total_copy(k, d))
            return carry

        lax.fori_loop(1, spans, step, 0)

    previous, own, following = blocks = [slice(i * OWN, (i + 1) * OWN) for i in range(3)]

    def send_contribs(k, image):
        for block in (0, 2, 1) if k < 2 else (0, 2):
            value = image(blocks[block])
            if k < 2:
                local_window[blocks[block], :] = value
            contrib_out[k, block] = value.astype(CONTRIB)
            if k == 0 and block == 0:
                pl.semaphore_wait(barrier, spans + chips - 1)
            for i in reversed(used_routes(k)):
                if routes[i][0] == block:
                    contrib_copy(k, i).start()
        if k == 2:
            local_window[own, :] = image(own)

    def receive_contribs(k):
        for i in used_routes(k):
            contrib_copy(k, i).wait_recv()

        def arrived(i):
            return contrib_in[k, i].astype(F32)

        v[k] = local_window[own, :] + arrived(2) + arrived(3)
        if k < 2:
            window[k, previous] = (local_window[previous, :] + arrived(0) + arrived(1)).astype(BF16)
            window[k, own] = v[k].astype(BF16)
            window[k, following] = (local_window[following, :] + arrived(4) + arrived(5)).astype(
                BF16
            )

    send_contribs(0, picked)

    place_t = as_column(place.astype(F32))

    def build_pick_t(j, carry):
        lanes = pl.ds(pl.multiple_of(j * CASES, CASES), CASES)
        at = lax.broadcasted_iota(jnp.int32, (SLOTS, CASES), 1) + j * CASES
        pick_t[:, lanes] = jnp.where(place_t == at.astype(F32), 1.0, 0.0).astype(BF16)
        return carry

    lax.fori_loop(0, SLOTS // CASES, build_pick_t, 0)
    loads[4].wait()
    reach = dot(pick[...], corner[...])
    high, low = two_parts(reach)
    corner_w[:, :CORNERS] = high
    corner_w[:, CORNERS:] = low
    high, low = two_parts(jnp.transpose(reach))
    corner_t[:, :SLOTS] = high
    corner_t[:, SLOTS:] = low
    loads[5].wait()
    loads[6].wait()

    receive_contribs(0)
    for k in range(2):
        w_part[k] = dot(corner_t[:, :SLOTS], window[k]) + dot(corner_t[:, SLOTS:], window[k])
        chip_copy(k).start()
        norm = column_sum(v[k] * v[k])
        u = dot(pick_t[...], window[k]).astype(BF16)
        y = dot(dual[...], u)
        ring_sums = sum_rows(norm, column_sum(u.astype(F32) * y))
        chip_copy(k).wait_recv()
        half = w_part[k, mine] + chip_in[k]
        ring_out[k, :HALF] = half.astype(BF16)
        ring_out[k, HALF:] = ring_sums.astype(BF16)
        for copy in ring_copies(k):
            copy.start()
        high, low = two_parts(y)
        split[:, :CASES] = high
        split[:, CASES:] = low
        for block in (previous, own, following):
            local_window[block, :] = picked(block)
        for copy in ring_copies(k):
            copy.wait_recv()
        for d in range(chips - 1):
            half = half + ring_in[k, d, :HALF].astype(F32)
            ring_sums = ring_sums + ring_in[k, d, HALF:].astype(F32)
        pair_out[k, :HALF] = half
        pair_out[k, HALF:] = ring_sums
        pair_copy(k).start()
        w_full[mine, :] = half
        pair_copy(k).wait_recv()
        w_full[theirs, :] = pair_in[k, :HALF]
        ring_sums = ring_sums + pair_in[k, HALF:]
        w = w_full[...]
        z = jnp.dot(stiff[...], w, precision=lax.Precision.HIGHEST, preferred_element_type=F32)
        z_narrow = z.astype(BF16)
        z_twice = jnp.concatenate([z_narrow, z_narrow], axis=0)

        def image(rows):
            return local_window[rows, :] + dot(corner_w[rows, :], z_twice)

        send_contribs(k + 1, image)
        coarse = column_sum(w * z_narrow.astype(F32))
        totals[k, 0] = jnp.concatenate(
            [column_sum(ring_sums[0:3]), column_sum(ring_sums[3:6]) + coarse], axis=0
        )
        each_total(k, lambda copy: copy.start())
        receive_contribs(k + 1)

    for k in range(2):
        each_total(k, lambda copy: copy.wait_recv())
    first = jnp.sum(totals[0], axis=0)
    second = jnp.sum(totals[1], axis=0)
    g00, g01 = first[0:1], first[1:2]
    g11, g12 = second[0:1], second[1:2]
    alpha0 = g00 / g01
    norm1 = g00 - 2.0 * alpha0 * g01 + alpha0 * alpha0 * g11
    beta = norm1 / g00
    grown = 1.0 + beta
    curve = grown * grown * g01 - 2.0 * grown * alpha0 * g11 + alpha0 * alpha0 * g12
    alpha1 = norm1 / curve
    v0, v1, v2 = v[0], v[1], v[2]
    residual1 = v0 - alpha0 * v1
    direction1 = residual1 + beta * v0
    solution_ref[...] = alpha0 * v0 + alpha1 * direction1
    residual_ref[...] = residual1 - alpha1 * (grown * v1 - alpha0 * v2)

    for k in range(3):
        for i in used_routes(k):
            contrib_copy(k, i).wait_send()
    for k in range(2):
        for copy in [chip_copy(k), pair_copy(k)] + ring_copies(k):
            copy.wait_send()
        each_total(k, lambda copy: copy.wait_send())


def solution(mesh):
    spans, subs = mesh.shape["span"], mesh.shape["sub"]
    chips = subs // 2
    vmem = pl.BlockSpec(memory_space=pltpu.VMEM)
    smem = pl.BlockSpec(memory_space=pltpu.SMEM)
    hbm = pl.BlockSpec(memory_space=pltpu.HBM)
    dma = pltpu.SemaphoreType.DMA

    def on_device(
        stress,
        history,
        retard,
        compliance,
        micro,
        lengths,
        multiplier_index,
        dual_block,
        corner_map,
        coarse_stiffness_inverse,
    ):
        units = history.shape[0]
        return pl.pallas_call(
            functools.partial(kernel, spans, subs),
            name="creep_step",
            out_shape=[jax.ShapeDtypeStruct((OWN, CASES), F32)] * 2,
            in_specs=[smem] * 3 + [hbm] * 7,
            out_specs=[vmem] * 2,
            scratch_shapes=[
                pltpu.VMEM((SLOTS, CASES), BF16),
                pltpu.VMEM((units, 1, SLOTS), F32),
                pltpu.VMEM((1, SLOTS), F32),
                pltpu.VMEM((1, SLOTS), jnp.int32),
                pltpu.VMEM((SLOTS, SLOTS), BF16),
                pltpu.VMEM((SLOTS, CORNERS), BF16),
                pltpu.VMEM((CORNERS, CORNERS), F32),
                pltpu.VMEM((SLOTS, SLOTS), BF16),
                pltpu.VMEM((SLOTS, SLOTS), BF16),
                pltpu.VMEM((CORNERS, 2 * SLOTS), BF16),
                pltpu.VMEM((SLOTS, 2 * CORNERS), BF16),
                pltpu.VMEM((SLOTS, 2 * CASES), BF16),
                pltpu.VMEM((2, SLOTS, CASES), BF16),
                pltpu.VMEM((SLOTS, CASES), F32),
                pltpu.VMEM((3, OWN, CASES), F32),
                pltpu.VMEM((3, 3, OWN, CASES), CONTRIB),
                pltpu.VMEM((3, 6, OWN, CASES), CONTRIB),
                pltpu.VMEM((2, CORNERS, CASES), F32),
                pltpu.VMEM((CORNERS, CASES), F32),
                pltpu.VMEM((2, HALF, CASES), F32),
                pltpu.VMEM((2, HALF + SUMS, CASES), BF16),
                pltpu.VMEM((2, chips - 1, HALF + SUMS, CASES), BF16),
                pltpu.VMEM((2, HALF + SUMS, CASES), F32),
                pltpu.VMEM((2, HALF + SUMS, CASES), F32),
                pltpu.VMEM((2, spans, 2, CASES), F32),
                dma((7,)),
                dma((3, 6)),
                dma((3, 6)),
                dma((2, 2)),
                dma((2, chips - 1)),
                dma((2, chips - 1)),
                dma((2, 2)),
                dma((2, spans)),
                dma((2, spans)),
            ],
            compiler_params=pltpu.CompilerParams(
                collective_id=0, has_side_effects=True, vmem_limit_bytes=60 * 2**20
            ),
        )(
            retard,
            compliance,
            lengths,
            stress,
            history,
            micro,
            multiplier_index,
            dual_block,
            corner_map,
            coarse_stiffness_inverse,
        )

    rows = P(("span", "sub"), None)
    blocks = P(("span", "sub"), None, None)
    return jax.shard_map(
        on_device,
        mesh=mesh,
        in_specs=(
            blocks,
            P(None, ("span", "sub"), None),
            P(),
            P(),
            rows,
            P(("span", "sub")),
            rows,
            blocks,
            blocks,
            P("span", None, None),
        ),
        out_specs=(rows, rows),
        check_vma=False,
    )
```

```python
import functools

import jax
import jax.numpy as jnp
from jax import lax
from jax.experimental import pallas as pl
from jax.experimental.pallas import tpu as pltpu
from jax.sharding import PartitionSpec as P

MESH = pl.DeviceIdType.MESH
F32 = jnp.float32
BF16 = jnp.bfloat16
CONTRIB = jnp.bfloat16
OWN = 256
SLOTS = 768
CASES = 128
CORNERS = 128
HALF = CORNERS // 2
SUMS = 16
ROWS = 64


def dot(a, b):
    return jnp.dot(a, b, preferred_element_type=F32)


def two_parts(x):
    high = x.astype(BF16)
    return high, (x - high.astype(F32)).astype(BF16)


def column_sum(x):
    return jnp.sum(x, axis=0, keepdims=True)


def as_column(row):
    return jnp.transpose(jnp.broadcast_to(row, (CASES, SLOTS)))


def sum_rows(first, second):
    row = lax.broadcasted_iota(jnp.int32, (SUMS, CASES), 0)
    out = jnp.zeros((SUMS, CASES), F32)
    for base, value in ((0, first), (3, second)):
        rest = value
        for i in range(3):
            part = rest.astype(BF16).astype(F32)
            rest = rest - part
            out = jnp.where(row == base + i, part, out)
    return out


def kernel(
    spans,
    subs,
    retard_hbm,
    compliance_hbm,
    lengths_hbm,
    stress_hbm,
    history_hbm,
    micro_hbm,
    index_hbm,
    dual_hbm,
    corner_hbm,
    stiff_hbm,
    basis0_hbm,
    basis1_hbm,
    basis2_hbm,
    factor0,
    factor1,
    retard,
    compliance,
    lengths,
    stress,
    history,
    micro,
    index,
    dual,
    corner,
    stiff,
    pick,
    pick_t,
    corner_t,
    corner_w,
    split,
    window,
    local_window,
    v,
    contrib_out,
    contrib_in,
    w_part,
    w_full,
    chip_in,
    ring_out,
    ring_in,
    pair_out,
    pair_in,
    totals,
    load_sem,
    keep_sem,
    contrib_send,
    contrib_recv,
    chip_sem,
    ring_sem,
    pair_sem,
    total_sem,
):
    p = lax.axis_index("span")
    s = lax.axis_index("sub")
    chips = subs // 2
    core = lax.rem(s, 2)
    partner = (p, s + 1 - 2 * core)
    mine = pl.ds(pl.multiple_of(core * HALF, HALF), HALF)
    theirs = pl.ds(pl.multiple_of((1 - core) * HALF, HALF), HALF)

    loads = [
        pltpu.make_async_copy(src, dst, load_sem.at[i])
        for i, (src, dst) in enumerate(
            (
                (lengths_hbm, lengths),
                (index_hbm, index),
                (retard_hbm, retard),
                (compliance_hbm, compliance),
                (micro_hbm, micro),
                (history_hbm, history),
                (stress_hbm.at[0], stress),
                (corner_hbm.at[0], corner),
                (dual_hbm.at[0], dual),
                (stiff_hbm.at[0], stiff),
            )
        )
    ]
    for copy in loads:
        copy.start()

    barrier = pltpu.get_barrier_semaphore()

    def greet_span(d, carry):
        pl.semaphore_signal(
            barrier, inc=1, device_id=(lax.rem(p + d, spans), s), device_id_type=MESH
        )
        return carry

    def greet_chip(d, carry):
        pl.semaphore_signal(
            barrier, inc=1, device_id=(p, lax.rem(s + 2 * d, subs)), device_id_type=MESH
        )
        return carry

    lax.fori_loop(1, spans, greet_span, 0)
    lax.fori_loop(1, chips, greet_chip, 0)
    pl.semaphore_signal(barrier, inc=1, device_id=partner, device_id_type=MESH)

    loads[0].wait()
    loads[1].wait()
    slot = lax.broadcasted_iota(jnp.int32, (1, SLOTS), 1)
    owner_span = index[...] // (OWN * subs)
    place = (owner_span - p + 1) * OWN + lax.rem(index[...], OWN)
    place = jnp.where(slot < lengths[0, 0], place, -1)

    def build_pick(i, carry):
        rows = pl.ds(pl.multiple_of(i * ROWS, ROWS), ROWS)
        at = lax.broadcasted_iota(jnp.int32, (ROWS, SLOTS), 0) + i * ROWS
        pick[rows, :] = jnp.where(at == place, 1.0, 0.0).astype(BF16)
        return carry

    lax.fori_loop(0, SLOTS // ROWS, build_pick, 0)

    for copy in loads[2:6]:
        copy.wait()
    creep = jnp.zeros((1, SLOTS), F32)
    past = jnp.zeros((1, SLOTS), F32)
    for k in range(history.shape[0]):
        weight = 1.0 - jnp.exp(-1.0 / jnp.full((1, SLOTS), retard[k], F32))
        creep = creep + weight * compliance[k]
        past = past + weight * history[k]
    relaxed = micro[...] / (1.0 + micro[...])
    scale = as_column(creep + 0.5 * relaxed)
    past = as_column(past)
    loads[6].wait()
    load = scale * stress[...].astype(F32) - past
    high, low = two_parts(load)
    split[:, :CASES] = high
    split[:, CASES:] = low

    def picked(rows):
        both = dot(pick[rows, :], split[...])
        return both[:, :CASES] + both[:, CASES:]

    routes = ((1, 1), (2, 2), (2, 1), (0, -1), (1, -1), (0, -2))

    def contrib_copy(k, i):
        block, onward = routes[i]
        return pltpu.make_async_remote_copy(
            src_ref=contrib_out.at[k, block],
            dst_ref=contrib_in.at[k, i],
            send_sem=contrib_send.at[k, i],
            recv_sem=contrib_recv.at[k, i],
            device_id=(lax.rem(p + spans + onward, spans), s),
            device_id_type=MESH,
        )

    def used_routes(k):
        return range(6) if k < 2 else (2, 3)

    def chip_copy(k):
        return pltpu.make_async_remote_copy(
            src_ref=w_part.at[k, theirs],
            dst_ref=chip_in.at[k],
            send_sem=chip_sem.at[k, 0],
            recv_sem=chip_sem.at[k, 1],
            device_id=partner,
            device_id_type=MESH,
        )

    def ring_copies(k):
        return [
            pltpu.make_async_remote_copy(
                src_ref=ring_out.at[k],
                dst_ref=ring_in.at[k, d - 1],
                send_sem=ring_sem.at[k, 0],
                recv_sem=ring_sem.at[k, 1],
                device_id=(p, lax.rem(s + 2 * d, subs)),
                device_id_type=MESH,
            )
            for d in range(1, chips)
        ]

    def all_ring(k):
        return pltpu.make_async_remote_copy(
            src_ref=ring_in.at[k],
            dst_ref=ring_in.at[k],
            send_sem=ring_sem.at[k, 0],
            recv_sem=ring_sem.at[k, 1],
            device_id=partner,
            device_id_type=MESH,
        )

    def pair_copy(k):
        return pltpu.make_async_remote_copy(
            src_ref=pair_out.at[k],
            dst_ref=pair_in.at[k],
            send_sem=pair_sem.at[k, 0],
            recv_sem=pair_sem.at[k, 1],
            device_id=partner,
            device_id_type=MESH,
        )

    def total_copy(k, d):
        return pltpu.make_async_remote_copy(
            src_ref=totals.at[k, 0],
            dst_ref=totals.at[k, d],
            send_sem=total_sem.at[k, 0],
            recv_sem=total_sem.at[k, 1],
            device_id=(lax.rem(p + d, spans), s),
            device_id_type=MESH,
        )

    def send_totals(k):
        def step(d, carry):
            total_copy(k, d).start()
            return carry

        lax.fori_loop(1, spans, step, 0)

    def all_totals(k):
        rest = totals.at[k, pl.ds(1, spans - 1)]
        return pltpu.make_async_remote_copy(
            src_ref=rest,
            dst_ref=rest,
            send_sem=total_sem.at[k, 0],
            recv_sem=total_sem.at[k, 1],
            device_id=partner,
            device_id_type=MESH,
        )

    previous, own, following = blocks = [slice(i * OWN, (i + 1) * OWN) for i in range(3)]

    def send_contribs(k, image):
        for block in (0, 2, 1) if k < 2 else (0, 2):
            value = image(blocks[block])
            if k < 2:
                local_window[blocks[block], :] = value
            contrib_out[k, block] = value.astype(CONTRIB)
            if k == 0 and block == 0:
                pl.semaphore_wait(barrier, spans + chips - 1)
            for i in reversed(used_routes(k)):
                if routes[i][0] == block:
                    contrib_copy(k, i).start()

    def receive_contribs(k):
        for i in used_routes(k):
            contrib_copy(k, i).wait_recv()

        def arrived(i):
            return contrib_in[k, i].astype(F32)

        v[k] = local_window[own, :] + arrived(2) + arrived(3)
        keeps[k].start()
        if k < 2:
            window[k, previous] = (local_window[previous, :] + arrived(0) + arrived(1)).astype(BF16)
            window[k, own] = v[k].astype(BF16)
            window[k, following] = (local_window[following, :] + arrived(4) + arrived(5)).astype(
                BF16
            )

    keeps = [
        pltpu.make_async_copy(v.at[k], out, keep_sem.at[k])
        for k, out in enumerate((basis0_hbm, basis1_hbm, basis2_hbm))
    ]
    send_contribs(0, picked)

    place_t = as_column(place.astype(F32))

    def build_pick_t(j, carry):
        lanes = pl.ds(pl.multiple_of(j * CASES, CASES), CASES)
        at = lax.broadcasted_iota(jnp.int32, (SLOTS, CASES), 1) + j * CASES
        pick_t[:, lanes] = jnp.where(place_t == at.astype(F32), 1.0, 0.0).astype(BF16)
        return carry

    lax.fori_loop(0, SLOTS // CASES, build_pick_t, 0)
    loads[7].wait()
    reach = dot(pick[...], corner[...])
    high, low = two_parts(reach)
    corner_w[:, :CORNERS] = high
    corner_w[:, CORNERS:] = low
    high, low = two_parts(jnp.transpose(reach))
    corner_t[:CORNERS, :] = high
    corner_t[CORNERS:, :] = low
    loads[8].wait()
    loads[9].wait()

    receive_contribs(0)
    for k in range(2):
        both = dot(corner_t[...], window[k])
        w_part[k] = both[:CORNERS] + both[CORNERS:]
        chip_copy(k).start()
        norm = column_sum(v[k] * v[k])
        u = dot(pick_t[...], window[k]).astype(BF16)
        y = dot(dual[...], u)
        ring_sums = sum_rows(norm, column_sum(u.astype(F32) * y))
        chip_copy(k).wait_recv()
        half = w_part[k, mine] + chip_in[k]
        ring_out[k, :HALF] = half.astype(BF16)
        ring_out[k, HALF:] = ring_sums.astype(BF16)
        for copy in ring_copies(k):
            copy.start()
        high, low = two_parts(y)
        split[:, :CASES] = high
        split[:, CASES:] = low
        for block in (previous, own, following):
            local_window[block, :] = picked(block)
        all_ring(k).wait_recv()
        for d in range(chips - 1):
            half = half + ring_in[k, d, :HALF].astype(F32)
            ring_sums = ring_sums + ring_in[k, d, HALF:].astype(F32)
        pair_out[k, :HALF] = half
        pair_out[k, HALF:] = ring_sums
        pair_copy(k).start()
        w_full[mine, :] = half
        pair_copy(k).wait_recv()
        w_full[theirs, :] = pair_in[k, :HALF]
        ring_sums = ring_sums + pair_in[k, HALF:]
        w = w_full[...]
        z = jnp.dot(stiff[...], w, precision=lax.Precision.HIGHEST, preferred_element_type=F32)
        z_narrow = z.astype(BF16)
        z_twice = jnp.concatenate([z_narrow, z_narrow], axis=0)

        def image(rows):
            return local_window[rows, :] + dot(corner_w[rows, :], z_twice)

        send_contribs(k + 1, image)
        coarse = column_sum(w * z_narrow.astype(F32))
        totals[k, 0] = jnp.concatenate(
            [column_sum(ring_sums[0:3]), column_sum(ring_sums[3:6]) + coarse], axis=0
        )
        send_totals(k)
        if k == 1:
            local_window[own, :] = image(own)
        receive_contribs(k + 1)

    for k in range(2):
        all_totals(k).wait_recv()
    first = jnp.sum(totals[0], axis=0)
    second = jnp.sum(totals[1], axis=0)
    g00, g01 = first[0:1], first[1:2]
    g11, g12 = second[0:1], second[1:2]
    alpha0 = g00 / g01
    norm1 = g00 - 2.0 * alpha0 * g01 + alpha0 * alpha0 * g11
    beta = norm1 / g00
    grown = 1.0 + beta
    curve = grown * grown * g01 - 2.0 * grown * alpha0 * g11 + alpha0 * alpha0 * g12
    alpha1 = norm1 / curve
    factor0[...] = alpha0 + alpha1 * grown
    factor1[...] = alpha0 * alpha1
    for copy in keeps:
        copy.wait()

    for k in range(3):
        for i in used_routes(k):
            contrib_copy(k, i).wait_send()
    for k in range(2):
        for copy in (chip_copy(k), pair_copy(k), all_ring(k)):
            copy.wait_send()
        all_totals(k).wait_send()


def solution(mesh):
    spans, subs = mesh.shape["span"], mesh.shape["sub"]
    chips = subs // 2
    vmem = pl.BlockSpec(memory_space=pltpu.VMEM)
    hbm = pl.BlockSpec(memory_space=pl.ANY)
    dma = pltpu.SemaphoreType.DMA

    def on_device(
        stress,
        history,
        retard,
        compliance,
        micro,
        lengths,
        multiplier_index,
        dual_block,
        corner_map,
        coarse_stiffness_inverse,
    ):
        units = history.shape[0]
        v0, v1, v2, first, second = pl.pallas_call(
            functools.partial(kernel, spans, subs),
            name="creep_step",
            out_shape=[jax.ShapeDtypeStruct((OWN, CASES), F32)] * 3
            + [jax.ShapeDtypeStruct((1, CASES), F32)] * 2,
            in_specs=[hbm] * 10,
            out_specs=[hbm] * 3 + [vmem] * 2,
            scratch_shapes=[
                pltpu.SMEM((units,), F32),
                pltpu.SMEM((units,), F32),
                pltpu.SMEM((1, 1), jnp.int32),
                pltpu.VMEM((SLOTS, CASES), BF16),
                pltpu.VMEM((units, 1, SLOTS), F32),
                pltpu.VMEM((1, SLOTS), F32),
                pltpu.VMEM((1, SLOTS), jnp.int32),
                pltpu.VMEM((SLOTS, SLOTS), BF16),
                pltpu.VMEM((SLOTS, CORNERS), BF16),
                pltpu.VMEM((CORNERS, CORNERS), F32),
                pltpu.VMEM((SLOTS, SLOTS), BF16),
                pltpu.VMEM((SLOTS, SLOTS), BF16),
                pltpu.VMEM((2 * CORNERS, SLOTS), BF16),
                pltpu.VMEM((SLOTS, 2 * CORNERS), BF16),
                pltpu.VMEM((SLOTS, 2 * CASES), BF16),
                pltpu.VMEM((2, SLOTS, CASES), BF16),
                pltpu.VMEM((SLOTS, CASES), F32),
                pltpu.VMEM((3, OWN, CASES), F32),
                pltpu.VMEM((3, 3, OWN, CASES), CONTRIB),
                pltpu.VMEM((3, 6, OWN, CASES), CONTRIB),
                pltpu.VMEM((2, CORNERS, CASES), F32),
                pltpu.VMEM((CORNERS, CASES), F32),
                pltpu.VMEM((2, HALF, CASES), F32),
                pltpu.VMEM((2, HALF + SUMS, CASES), BF16),
                pltpu.VMEM((2, chips - 1, HALF + SUMS, CASES), BF16),
                pltpu.VMEM((2, HALF + SUMS, CASES), F32),
                pltpu.VMEM((2, HALF + SUMS, CASES), F32),
                pltpu.VMEM((2, spans, 2, CASES), F32),
                dma((10,)),
                dma((3,)),
                dma((3, 6)),
                dma((3, 6)),
                dma((2, 2)),
                dma((2, 2)),
                dma((2, 2)),
                dma((2, 2)),
            ],
            compiler_params=pltpu.CompilerParams(
                collective_id=0, has_side_effects=True, vmem_limit_bytes=60 * 2**20
            ),
        )(
            retard,
            compliance,
            lengths.reshape(1, 1),
            stress,
            history,
            micro,
            multiplier_index,
            dual_block,
            corner_map,
            coarse_stiffness_inverse,
        )
        return first * v0 - second * v1, v0 - first * v1 + second * v2

    rows = P(("span", "sub"), None)
    blocks = P(("span", "sub"), None, None)
    return jax.shard_map(
        on_device,
        mesh=mesh,
        in_specs=(
            blocks,
            P(None, ("span", "sub"), None),
            P(),
            P(),
            rows,
            P(("span", "sub")),
            rows,
            blocks,
            blocks,
            P("span", None, None),
        ),
        out_specs=(rows, rows),
        check_vma=False,
    )
```

```python
import functools

import jax
import jax.numpy as jnp
from jax import lax
from jax.experimental import pallas as pl
from jax.experimental.pallas import tpu as pltpu
from jax.sharding import PartitionSpec as P

MESH = pl.DeviceIdType.MESH
F32 = jnp.float32
BF16 = jnp.bfloat16
CONTRIB = jnp.bfloat16
OWN = 256
SLOTS = 768
CASES = 128
CORNERS = 128
HALF = CORNERS // 2
SUMS = 16
ROWS = 64


def dot(a, b):
    return jnp.dot(a, b, preferred_element_type=F32)


def two_parts(x):
    high = x.astype(BF16)
    return high, (x - high.astype(F32)).astype(BF16)


def column_sum(x):
    return jnp.sum(x, axis=0, keepdims=True)


def as_column(row):
    return jnp.transpose(jnp.broadcast_to(row, (CASES, SLOTS)))


def sum_rows(first, second):
    row = lax.broadcasted_iota(jnp.int32, (SUMS, CASES), 0)
    out = jnp.zeros((SUMS, CASES), F32)
    for base, value in ((0, first), (3, second)):
        rest = value
        for i in range(3):
            part = rest.astype(BF16).astype(F32)
            rest = rest - part
            out = jnp.where(row == base + i, part, out)
    return out


def kernel(
    spans,
    subs,
    retard_hbm,
    compliance_hbm,
    lengths_hbm,
    stress_hbm,
    history_hbm,
    micro_hbm,
    index_hbm,
    dual_hbm,
    corner_hbm,
    stiff_hbm,
    basis0_hbm,
    basis1_hbm,
    basis2_hbm,
    factor0,
    factor1,
    retard,
    compliance,
    lengths,
    stress,
    history,
    micro,
    index,
    dual,
    corner,
    stiff,
    pick,
    pick_t,
    corner_t,
    corner_w,
    coarse,
    w_near,
    split,
    window,
    local_window,
    v,
    contrib_out,
    contrib_in,
    w_part,
    w_full,
    chip_in,
    ring_out,
    ring_in,
    pair_out,
    pair_in,
    totals,
    load_sem,
    keep_sem,
    contrib_send,
    contrib_recv,
    coarse_send,
    coarse_recv,
    near_send,
    near_recv,
    chip_sem,
    ring_sem,
    pair_sem,
    total_sem,
):
    p = lax.axis_index("span")
    s = lax.axis_index("sub")
    chips = subs // 2
    core = lax.rem(s, 2)
    partner = (p, s + 1 - 2 * core)
    mine = pl.ds(pl.multiple_of(core * HALF, HALF), HALF)
    theirs = pl.ds(pl.multiple_of((1 - core) * HALF, HALF), HALF)

    loads = [
        pltpu.make_async_copy(src, dst, load_sem.at[i])
        for i, (src, dst) in enumerate(
            (
                (lengths_hbm, lengths),
                (index_hbm, index),
                (retard_hbm, retard),
                (compliance_hbm, compliance),
                (micro_hbm, micro),
                (history_hbm, history),
                (stress_hbm.at[0], stress),
                (corner_hbm.at[0], corner),
                (dual_hbm.at[0], dual),
                (stiff_hbm.at[0], stiff),
            )
        )
    ]
    for copy in loads:
        copy.start()

    barrier = pltpu.get_barrier_semaphore()

    def greet_span(d, carry):
        pl.semaphore_signal(
            barrier, inc=1, device_id=(lax.rem(p + d, spans), s), device_id_type=MESH
        )
        return carry

    def greet_chip(d, carry):
        pl.semaphore_signal(
            barrier, inc=1, device_id=(p, lax.rem(s + 2 * d, subs)), device_id_type=MESH
        )
        return carry

    pl.semaphore_signal(barrier, inc=1, device_id=partner, device_id_type=MESH)
    for d in (1, spans - 1, 2, spans - 2):
        greet_span(d, 0)
        pl.semaphore_signal(
            barrier, inc=1, device_id=(lax.rem(p + d, spans), partner[1]), device_id_type=MESH
        )
    lax.fori_loop(1, chips, greet_chip, 0)
    lax.fori_loop(3, spans - 2, greet_span, 0)

    loads[0].wait()
    loads[1].wait()
    slot = lax.broadcasted_iota(jnp.int32, (1, SLOTS), 1)
    owner_span = index[...] // (OWN * subs)
    place = (owner_span - p + 1) * OWN + lax.rem(index[...], OWN)
    place = jnp.where(slot < lengths[0, 0], place, -1)

    def build_pick(i, carry):
        rows = pl.ds(pl.multiple_of(i * ROWS, ROWS), ROWS)
        at = lax.broadcasted_iota(jnp.int32, (ROWS, SLOTS), 0) + i * ROWS
        pick[rows, :] = jnp.where(at == place, 1.0, 0.0).astype(BF16)
        return carry

    lax.fori_loop(0, SLOTS // ROWS, build_pick, 0)

    for copy in loads[2:6]:
        copy.wait()
    creep = jnp.zeros((1, SLOTS), F32)
    past = jnp.zeros((1, SLOTS), F32)
    for k in range(history.shape[0]):
        weight = 1.0 - jnp.exp(-1.0 / jnp.full((1, SLOTS), retard[k], F32))
        creep = creep + weight * compliance[k]
        past = past + weight * history[k]
    relaxed = micro[...] / (1.0 + micro[...])
    scale = as_column(creep + 0.5 * relaxed)
    past = as_column(past)
    loads[6].wait()
    load = scale * stress[...].astype(F32) - past
    high, low = two_parts(load)
    split[:, :CASES] = high
    split[:, CASES:] = low

    def picked(rows):
        both = dot(pick[rows, :], split[...])
        return both[:, :CASES] + both[:, CASES:]

    routes = ((1, 1), (2, 2), (2, 1), (0, -1), (1, -1), (0, -2))

    def contrib_copy(k, i):
        block, onward = routes[i]
        return pltpu.make_async_remote_copy(
            src_ref=contrib_out.at[k, block],
            dst_ref=contrib_in.at[k, i],
            send_sem=contrib_send.at[k, i],
            recv_sem=contrib_recv.at[k, i],
            device_id=(lax.rem(p + spans + onward, spans), s),
            device_id_type=MESH,
        )

    landing = ((0, 1), (0, 0), (1, 0), (1, 2), (2, 1), (2, 2))

    def coarse_copy(i):
        block, onward = routes[i]
        row, column = landing[i]
        return pltpu.make_async_remote_copy(
            src_ref=coarse.at[pl.ds(block * OWN, OWN), pl.ds((2 - block) * CORNERS, CORNERS)],
            dst_ref=coarse.at[pl.ds(row * OWN, OWN), pl.ds(column * CORNERS, CORNERS)],
            send_sem=coarse_send.at[i],
            recv_sem=coarse_recv.at[i],
            device_id=(lax.rem(p + spans + onward, spans), s),
            device_id_type=MESH,
        )

    def near_copies():
        kept = w_near.at[pl.ds(pl.multiple_of(2 * CORNERS + core * HALF, HALF), HALF)]
        copies = []
        for onward in (2, -2, 1, -1):
            place = pl.multiple_of((2 - onward) * CORNERS + core * HALF, HALF)
            for to in (s, partner[1]):
                copies.append(
                    pltpu.make_async_remote_copy(
                        src_ref=kept,
                        dst_ref=w_near.at[pl.ds(place, HALF)],
                        send_sem=near_send.at[len(copies)],
                        recv_sem=near_recv.at[0 if onward > 0 else 1],
                        device_id=(lax.rem(p + spans + onward, spans), to),
                        device_id_type=MESH,
                    )
                )
        return copies

    def all_near(side):
        rows = w_near.at[pl.ds(side * 3 * CORNERS, 2 * CORNERS)]
        return pltpu.make_async_remote_copy(
            src_ref=rows,
            dst_ref=rows,
            send_sem=near_send.at[0],
            recv_sem=near_recv.at[side],
            device_id=partner,
            device_id_type=MESH,
        )

    def used_routes(k):
        return range(6) if k < 2 else (2, 3)

    def chip_copy(k):
        return pltpu.make_async_remote_copy(
            src_ref=w_part.at[k, theirs],
            dst_ref=chip_in.at[k],
            send_sem=chip_sem.at[k, 0],
            recv_sem=chip_sem.at[k, 1],
            device_id=partner,
            device_id_type=MESH,
        )

    def ring_copies(k):
        return [
            pltpu.make_async_remote_copy(
                src_ref=ring_out.at[k],
                dst_ref=ring_in.at[k, d - 1],
                send_sem=ring_sem.at[k, 0],
                recv_sem=ring_sem.at[k, 1],
                device_id=(p, lax.rem(s + 2 * d, subs)),
                device_id_type=MESH,
            )
            for d in range(1, chips)
        ]

    def all_ring(k):
        return pltpu.make_async_remote_copy(
            src_ref=ring_in.at[k],
            dst_ref=ring_in.at[k],
            send_sem=ring_sem.at[k, 0],
            recv_sem=ring_sem.at[k, 1],
            device_id=partner,
            device_id_type=MESH,
        )

    def pair_copy(k):
        return pltpu.make_async_remote_copy(
            src_ref=pair_out.at[k],
            dst_ref=pair_in.at[k],
            send_sem=pair_sem.at[k, 0],
            recv_sem=pair_sem.at[k, 1],
            device_id=partner,
            device_id_type=MESH,
        )

    def total_copy(k, d):
        return pltpu.make_async_remote_copy(
            src_ref=totals.at[k, 0],
            dst_ref=totals.at[k, d],
            send_sem=total_sem.at[k, 0],
            recv_sem=total_sem.at[k, 1],
            device_id=(lax.rem(p + d, spans), s),
            device_id_type=MESH,
        )

    def send_totals(k):
        def step(d, carry):
            total_copy(k, d).start()
            return carry

        lax.fori_loop(1, spans, step, 0)

    def all_totals(k):
        rest = totals.at[k, pl.ds(1, spans - 1)]
        return pltpu.make_async_remote_copy(
            src_ref=rest,
            dst_ref=rest,
            send_sem=total_sem.at[k, 0],
            recv_sem=total_sem.at[k, 1],
            device_id=partner,
            device_id_type=MESH,
        )

    previous, own, following = blocks = [slice(i * OWN, (i + 1) * OWN) for i in range(3)]

    def send_contribs(k, image):
        for block in (0, 2, 1) if k < 2 else (0, 2):
            value = image(blocks[block])
            if k < 2:
                local_window[blocks[block], :] = value
            contrib_out[k, block] = value.astype(CONTRIB)
            if k == 0 and block == 0:
                pl.semaphore_wait(barrier, spans + chips + 3)
            for i in reversed(used_routes(k)):
                if routes[i][0] == block:
                    contrib_copy(k, i).start()

    def receive_contribs(k):
        for i in used_routes(k):
            contrib_copy(k, i).wait_recv()

        def arrived(i):
            return contrib_in[k, i].astype(F32)

        if k == 1:
            for i in used_routes(k):
                coarse_copy(i).wait_recv()
            for side in range(2):
                all_near(side).wait_recv()
            for block in range(3):
                near = w_near[block * CORNERS : (block + 3) * CORNERS, :]
                local_window[blocks[block], :] += dot(coarse[blocks[block], :], near)
        v[k] = local_window[own, :] + arrived(2) + arrived(3)
        keeps[k].start()
        if k < 2:
            window[k, previous] = (local_window[previous, :] + arrived(0) + arrived(1)).astype(BF16)
            window[k, own] = v[k].astype(BF16)
            window[k, following] = (local_window[following, :] + arrived(4) + arrived(5)).astype(
                BF16
            )

    keeps = [
        pltpu.make_async_copy(v.at[k], out, keep_sem.at[k])
        for k, out in enumerate((basis0_hbm, basis1_hbm, basis2_hbm))
    ]
    send_contribs(0, picked)

    loads[7].wait()
    reach = dot(pick[...], corner[...])
    loads[9].wait()
    spread = jnp.dot(reach, stiff[...], precision=lax.Precision.HIGHEST, preferred_element_type=F32)
    for block in range(3):
        coarse[blocks[block], (2 - block) * CORNERS : (3 - block) * CORNERS] = spread[
            blocks[block]
        ].astype(BF16)

    for i in reversed(used_routes(0)):
        coarse_copy(i).start()
    high, low = two_parts(reach)
    corner_w[:, :CORNERS] = high
    corner_w[:, CORNERS:] = low
    high, low = two_parts(jnp.transpose(reach))
    corner_t[:CORNERS, :] = high
    corner_t[CORNERS:, :] = low
    place_t = as_column(place.astype(F32))

    def build_pick_t(j, carry):
        lanes = pl.ds(pl.multiple_of(j * CASES, CASES), CASES)
        at = lax.broadcasted_iota(jnp.int32, (SLOTS, CASES), 1) + j * CASES
        pick_t[:, lanes] = jnp.where(place_t == at.astype(F32), 1.0, 0.0).astype(BF16)
        return carry

    lax.fori_loop(0, SLOTS // CASES, build_pick_t, 0)
    loads[8].wait()
    receive_contribs(0)
    for k in range(2):
        both = dot(corner_t[...], window[k])
        w_part[k] = both[:CORNERS] + both[CORNERS:]
        chip_copy(k).start()
        norm = column_sum(v[k] * v[k])
        u = dot(pick_t[...], window[k]).astype(BF16)
        y = dot(dual[...], u)
        ring_sums = sum_rows(norm, column_sum(u.astype(F32) * y))
        chip_copy(k).wait_recv()
        half = w_part[k, mine] + chip_in[k]
        ring_out[k, :HALF] = half.astype(BF16)
        ring_out[k, HALF:] = ring_sums.astype(BF16)
        for copy in ring_copies(k):
            copy.start()
        high, low = two_parts(y)
        split[:, :CASES] = high
        split[:, CASES:] = low
        if k == 0:
            send_contribs(1, picked)
        else:
            for block in blocks:
                local_window[block, :] = picked(block)
        all_ring(k).wait_recv()
        for d in range(chips - 1):
            half = half + ring_in[k, d, :HALF].astype(F32)
            ring_sums = ring_sums + ring_in[k, d, HALF:].astype(F32)
        pair_out[k, :HALF] = half
        pair_out[k, HALF:] = ring_sums
        pair_copy(k).start()
        if k == 0:
            w_near[pl.ds(pl.multiple_of(2 * CORNERS + core * HALF, HALF), HALF), :] = half.astype(
                BF16
            )
            for copy in near_copies():
                copy.start()
        w_full[mine, :] = half
        pair_copy(k).wait_recv()
        w_full[theirs, :] = pair_in[k, :HALF]
        if k == 0:
            w_near[pl.ds(pl.multiple_of(3 * CORNERS - HALF - core * HALF, HALF), HALF), :] = pair_in[
                k, :HALF
            ].astype(BF16)
        ring_sums = ring_sums + pair_in[k, HALF:]
        w = w_full[...]
        z = jnp.dot(stiff[...], w, precision=lax.Precision.HIGHEST, preferred_element_type=F32)
        z_narrow = z.astype(BF16)
        z_twice = jnp.concatenate([z_narrow, z_narrow], axis=0)

        def image(rows):
            return local_window[rows, :] + dot(corner_w[rows, :], z_twice)

        if k == 1:
            send_contribs(2, image)
        energy = column_sum(w * z_narrow.astype(F32))
        totals[k, 0] = jnp.concatenate(
            [column_sum(ring_sums[0:3]), column_sum(ring_sums[3:6]) + energy], axis=0
        )
        send_totals(k)
        if k == 1:
            local_window[own, :] = image(own)
        receive_contribs(k + 1)

    for k in range(2):
        all_totals(k).wait_recv()
    first = jnp.sum(totals[0], axis=0)
    second = jnp.sum(totals[1], axis=0)
    g00, g01 = first[0:1], first[1:2]
    g11, g12 = second[0:1], second[1:2]
    alpha0 = g00 / g01
    norm1 = g00 - 2.0 * alpha0 * g01 + alpha0 * alpha0 * g11
    beta = norm1 / g00
    grown = 1.0 + beta
    curve = grown * grown * g01 - 2.0 * grown * alpha0 * g11 + alpha0 * alpha0 * g12
    alpha1 = norm1 / curve
    factor0[...] = alpha0 + alpha1 * grown
    factor1[...] = alpha0 * alpha1
    for copy in keeps:
        copy.wait()

    tail = near_copies() + [coarse_copy(i) for i in range(6)]
    for k in range(3):
        for i in used_routes(k):
            contrib_copy(k, i).wait_send()
    for k in range(2):
        for copy in [chip_copy(k), pair_copy(k), all_ring(k)] + (tail if k == 0 else []):
            copy.wait_send()
        all_totals(k).wait_send()


def solution(mesh):
    spans, subs = mesh.shape["span"], mesh.shape["sub"]
    chips = subs // 2
    vmem = pl.BlockSpec(memory_space=pltpu.VMEM)
    hbm = pl.BlockSpec(memory_space=pl.ANY)
    dma = pltpu.SemaphoreType.DMA

    def on_device(
        stress,
        history,
        retard,
        compliance,
        micro,
        lengths,
        multiplier_index,
        dual_block,
        corner_map,
        coarse_stiffness_inverse,
    ):
        units = history.shape[0]
        v0, v1, v2, first, second = pl.pallas_call(
            functools.partial(kernel, spans, subs),
            name="creep_step",
            out_shape=[jax.ShapeDtypeStruct((OWN, CASES), F32)] * 3
            + [jax.ShapeDtypeStruct((1, CASES), F32)] * 2,
            in_specs=[hbm] * 10,
            out_specs=[hbm] * 3 + [vmem] * 2,
            scratch_shapes=[
                pltpu.SMEM((units,), F32),
                pltpu.SMEM((units,), F32),
                pltpu.SMEM((1, 1), jnp.int32),
                pltpu.VMEM((SLOTS, CASES), BF16),
                pltpu.VMEM((units, 1, SLOTS), F32),
                pltpu.VMEM((1, SLOTS), F32),
                pltpu.VMEM((1, SLOTS), jnp.int32),
                pltpu.VMEM((SLOTS, SLOTS), BF16),
                pltpu.VMEM((SLOTS, CORNERS), BF16),
                pltpu.VMEM((CORNERS, CORNERS), F32),
                pltpu.VMEM((SLOTS, SLOTS), BF16),
                pltpu.VMEM((SLOTS, SLOTS), BF16),
                pltpu.VMEM((2 * CORNERS, SLOTS), BF16),
                pltpu.VMEM((SLOTS, 2 * CORNERS), BF16),
                pltpu.VMEM((SLOTS, 3 * CORNERS), BF16),
                pltpu.VMEM((5 * CORNERS, CASES), BF16),
                pltpu.VMEM((SLOTS, 2 * CASES), BF16),
                pltpu.VMEM((2, SLOTS, CASES), BF16),
                pltpu.VMEM((SLOTS, CASES), F32),
                pltpu.VMEM((3, OWN, CASES), F32),
                pltpu.VMEM((3, 3, OWN, CASES), CONTRIB),
                pltpu.VMEM((3, 6, OWN, CASES), CONTRIB),
                pltpu.VMEM((2, CORNERS, CASES), F32),
                pltpu.VMEM((CORNERS, CASES), F32),
                pltpu.VMEM((2, HALF, CASES), F32),
                pltpu.VMEM((2, HALF + SUMS, CASES), BF16),
                pltpu.VMEM((2, chips - 1, HALF + SUMS, CASES), BF16),
                pltpu.VMEM((2, HALF + SUMS, CASES), F32),
                pltpu.VMEM((2, HALF + SUMS, CASES), F32),
                pltpu.VMEM((2, spans, 2, CASES), F32),
                dma((10,)),
                dma((3,)),
                dma((3, 6)),
                dma((3, 6)),
                dma((6,)),
                dma((6,)),
                dma((8,)),
                dma((2,)),
                dma((2, 2)),
                dma((2, 2)),
                dma((2, 2)),
                dma((2, 2)),
            ],
            compiler_params=pltpu.CompilerParams(
                collective_id=0, has_side_effects=True, vmem_limit_bytes=60 * 2**20
            ),
        )(
            retard,
            compliance,
            lengths.reshape(1, 1),
            stress,
            history,
            micro,
            multiplier_index,
            dual_block,
            corner_map,
            coarse_stiffness_inverse,
        )
        return first * v0 - second * v1, v0 - first * v1 + second * v2

    rows = P(("span", "sub"), None)
    blocks = P(("span", "sub"), None, None)
    return jax.shard_map(
        on_device,
        mesh=mesh,
        in_specs=(
            blocks,
            P(None, ("span", "sub"), None),
            P(),
            P(),
            rows,
            P(("span", "sub")),
            rows,
            blocks,
            blocks,
            P("span", None, None),
        ),
        out_specs=(rows, rows),
        check_vma=False,
    )
```

```python
import functools

import jax
import jax.numpy as jnp
from jax import lax
from jax.experimental import pallas as pl
from jax.experimental.pallas import tpu as pltpu
from jax.sharding import PartitionSpec as P

MESH = pl.DeviceIdType.MESH
F32 = jnp.float32
BF16 = jnp.bfloat16
CONTRIB = jnp.bfloat16
OWN = 256
SLOTS = 768
CASES = 128
CORNERS = 128
HALF = CORNERS // 2
SUMS = 16
ROWS = 64


def dot(a, b):
    return jnp.dot(a, b, preferred_element_type=F32)


def two_parts(x):
    high = x.astype(BF16)
    return high, (x - high.astype(F32)).astype(BF16)


def column_sum(x):
    return jnp.sum(x, axis=0, keepdims=True)


def as_column(row):
    return jnp.transpose(jnp.broadcast_to(row, (CASES, SLOTS)))


def sum_rows(first, second):
    row = lax.broadcasted_iota(jnp.int32, (SUMS, CASES), 0)
    out = jnp.zeros((SUMS, CASES), F32)
    for base, value in ((0, first), (3, second)):
        rest = value
        for i in range(3):
            part = rest.astype(BF16).astype(F32)
            rest = rest - part
            out = jnp.where(row == base + i, part, out)
    return out


def kernel(
    spans,
    subs,
    retard_hbm,
    compliance_hbm,
    lengths_hbm,
    stress_hbm,
    history_hbm,
    micro_hbm,
    index_hbm,
    dual_hbm,
    corner_hbm,
    stiff_hbm,
    basis0_hbm,
    basis1_hbm,
    basis2_hbm,
    factor0,
    factor1,
    retard,
    compliance,
    lengths,
    stress,
    history,
    micro,
    index,
    dual,
    corner,
    stiff,
    pick,
    pick_t,
    corner_t,
    corner_w,
    coarse,
    w_near,
    split,
    window,
    local_window,
    v,
    contrib_out,
    contrib_in,
    w_part,
    w_full,
    chip_in,
    ring_out,
    ring_in,
    pair_out,
    pair_in,
    totals,
    load_sem,
    keep_sem,
    contrib_send,
    contrib_recv,
    coarse_send,
    coarse_recv,
    near_send,
    near_recv,
    chip_sem,
    ring_sem,
    pair_sem,
    total_sem,
):
    p = lax.axis_index("span")
    s = lax.axis_index("sub")
    chips = subs // 2
    core = lax.rem(s, 2)
    partner = (p, s + 1 - 2 * core)
    mine = pl.ds(pl.multiple_of(core * HALF, HALF), HALF)
    theirs = pl.ds(pl.multiple_of((1 - core) * HALF, HALF), HALF)

    loads = [
        pltpu.make_async_copy(src, dst, load_sem.at[i])
        for i, (src, dst) in enumerate(
            (
                (lengths_hbm, lengths),
                (index_hbm, index),
                (retard_hbm, retard),
                (compliance_hbm, compliance),
                (micro_hbm, micro),
                (history_hbm, history),
                (stress_hbm.at[0], stress),
                (corner_hbm.at[0], corner),
                (dual_hbm.at[0], dual),
                (stiff_hbm.at[0], stiff),
            )
        )
    ]
    for copy in loads:
        copy.start()

    barrier = pltpu.get_barrier_semaphore()

    def greet_span(d, carry):
        pl.semaphore_signal(
            barrier, inc=1, device_id=(lax.rem(p + d, spans), s), device_id_type=MESH
        )
        return carry

    def greet_chip(d, carry):
        pl.semaphore_signal(
            barrier, inc=1, device_id=(p, lax.rem(s + 2 * d, subs)), device_id_type=MESH
        )
        return carry

    pl.semaphore_signal(barrier, inc=1, device_id=partner, device_id_type=MESH)
    for d in (1, spans - 1, 2, spans - 2):
        greet_span(d, 0)
        pl.semaphore_signal(
            barrier, inc=1, device_id=(lax.rem(p + d, spans), partner[1]), device_id_type=MESH
        )
    lax.fori_loop(1, chips, greet_chip, 0)
    lax.fori_loop(3, spans - 2, greet_span, 0)

    loads[0].wait()
    loads[1].wait()
    slot = lax.broadcasted_iota(jnp.int32, (1, SLOTS), 1)
    owner_span = index[...] // (OWN * subs)
    place = (owner_span - p + 1) * OWN + lax.rem(index[...], OWN)
    place = jnp.where(slot < lengths[0, 0], place, -1)

    def build_pick(i, carry):
        rows = pl.ds(pl.multiple_of(i * ROWS, ROWS), ROWS)
        at = lax.broadcasted_iota(jnp.int32, (ROWS, SLOTS), 0) + i * ROWS
        pick[rows, :] = jnp.where(at == place, 1.0, 0.0).astype(BF16)
        return carry

    lax.fori_loop(0, SLOTS // ROWS, build_pick, 0)

    for copy in loads[2:6]:
        copy.wait()
    creep = jnp.zeros((1, SLOTS), F32)
    past = jnp.zeros((1, SLOTS), F32)
    for k in range(history.shape[0]):
        weight = 1.0 - jnp.exp(-1.0 / jnp.full((1, SLOTS), retard[k], F32))
        creep = creep + weight * compliance[k]
        past = past + weight * history[k]
    relaxed = micro[...] / (1.0 + micro[...])
    scale = as_column(creep + 0.5 * relaxed)
    past = as_column(past)
    loads[6].wait()
    load = scale * stress[...].astype(F32) - past
    high, low = two_parts(load)
    split[:, :CASES] = high
    split[:, CASES:] = low

    def picked(rows):
        both = dot(pick[rows, :], split[...])
        return both[:, :CASES] + both[:, CASES:]

    routes = ((1, 1), (2, 2), (2, 1), (0, -1), (1, -1), (0, -2))

    def contrib_copy(k, i):
        block, onward = routes[i]
        return pltpu.make_async_remote_copy(
            src_ref=contrib_out.at[k, block],
            dst_ref=contrib_in.at[k, i],
            send_sem=contrib_send.at[k, i],
            recv_sem=contrib_recv.at[k, i],
            device_id=(lax.rem(p + spans + onward, spans), s),
            device_id_type=MESH,
        )

    landing = ((0, 1), (0, 0), (1, 0), (1, 2), (2, 1), (2, 2))

    def coarse_copy(i):
        block, onward = routes[i]
        row, column = landing[i]
        return pltpu.make_async_remote_copy(
            src_ref=coarse.at[pl.ds(block * OWN, OWN), pl.ds((2 - block) * CORNERS, CORNERS)],
            dst_ref=coarse.at[pl.ds(row * OWN, OWN), pl.ds(column * CORNERS, CORNERS)],
            send_sem=coarse_send.at[i],
            recv_sem=coarse_recv.at[i],
            device_id=(lax.rem(p + spans + onward, spans), s),
            device_id_type=MESH,
        )

    def near_copies():
        kept = w_near.at[pl.ds(pl.multiple_of(2 * CORNERS + core * HALF, HALF), HALF)]
        copies = []
        for onward in (2, -2, 1, -1):
            place = pl.multiple_of((2 - onward) * CORNERS + core * HALF, HALF)
            for to in (s, partner[1]):
                copies.append(
                    pltpu.make_async_remote_copy(
                        src_ref=kept,
                        dst_ref=w_near.at[pl.ds(place, HALF)],
                        send_sem=near_send.at[len(copies)],
                        recv_sem=near_recv.at[0 if onward > 0 else 1],
                        device_id=(lax.rem(p + spans + onward, spans), to),
                        device_id_type=MESH,
                    )
                )
        return copies

    def all_near(side):
        rows = w_near.at[pl.ds(side * 3 * CORNERS, 2 * CORNERS)]
        return pltpu.make_async_remote_copy(
            src_ref=rows,
            dst_ref=rows,
            send_sem=near_send.at[0],
            recv_sem=near_recv.at[side],
            device_id=partner,
            device_id_type=MESH,
        )

    def used_routes(k):
        return range(6) if k < 2 else (2, 3)

    def chip_copy(k):
        return pltpu.make_async_remote_copy(
            src_ref=w_part.at[k, theirs],
            dst_ref=chip_in.at[k],
            send_sem=chip_sem.at[k, 0],
            recv_sem=chip_sem.at[k, 1],
            device_id=partner,
            device_id_type=MESH,
        )

    def ring_copies(k):
        return [
            pltpu.make_async_remote_copy(
                src_ref=ring_out.at[k],
                dst_ref=ring_in.at[k, d - 1],
                send_sem=ring_sem.at[k, 0],
                recv_sem=ring_sem.at[k, 1],
                device_id=(p, lax.rem(s + 2 * d, subs)),
                device_id_type=MESH,
            )
            for d in sorted(range(1, chips), key=lambda d: -min(d, chips - d))
        ]

    def all_ring(k):
        return pltpu.make_async_remote_copy(
            src_ref=ring_in.at[k],
            dst_ref=ring_in.at[k],
            send_sem=ring_sem.at[k, 0],
            recv_sem=ring_sem.at[k, 1],
            device_id=partner,
            device_id_type=MESH,
        )

    def pair_copy(k):
        return pltpu.make_async_remote_copy(
            src_ref=pair_out.at[k],
            dst_ref=pair_in.at[k],
            send_sem=pair_sem.at[k, 0],
            recv_sem=pair_sem.at[k, 1],
            device_id=partner,
            device_id_type=MESH,
        )

    def send_totals():
        def step(i, carry):
            d = 1 + lax.rem(i + spans // 3, spans - 1)
            pltpu.make_async_remote_copy(
                src_ref=totals.at[0],
                dst_ref=totals.at[d],
                send_sem=total_sem.at[0],
                recv_sem=total_sem.at[1],
                device_id=(lax.rem(p + d, spans), s),
                device_id_type=MESH,
            ).start()
            return carry

        lax.fori_loop(0, spans - 1, step, 0)

    def all_totals():
        rest = totals.at[pl.ds(1, spans - 1)]
        return pltpu.make_async_remote_copy(
            src_ref=rest,
            dst_ref=rest,
            send_sem=total_sem.at[0],
            recv_sem=total_sem.at[1],
            device_id=partner,
            device_id_type=MESH,
        )

    previous, own, following = blocks = [slice(i * OWN, (i + 1) * OWN) for i in range(3)]

    def send_contribs(k, image):
        for block in (0, 2, 1) if k < 2 else (0, 2):
            value = image(blocks[block])
            if k < 2:
                local_window[blocks[block], :] = value
            contrib_out[k, block] = value.astype(CONTRIB)
            if k == 0 and block == 0:
                pl.semaphore_wait(barrier, spans + chips + 3)
            for i in sorted(used_routes(k), key=lambda i: -abs(routes[i][1])):
                if routes[i][0] == block:
                    contrib_copy(k, i).start()

    def receive_contribs(k):
        for i in used_routes(k):
            contrib_copy(k, i).wait_recv()

        def arrived(i):
            return contrib_in[k, i].astype(F32)

        if k == 1:
            for i in used_routes(k):
                coarse_copy(i).wait_recv()
            for side in range(2):
                all_near(side).wait_recv()
            for block in range(3):
                near = w_near[block * CORNERS : (block + 3) * CORNERS, :]
                local_window[blocks[block], :] += dot(coarse[blocks[block], :], near)
        v[k] = local_window[own, :] + arrived(2) + arrived(3)
        keeps[k].start()
        if k < 2:
            window[k, previous] = (local_window[previous, :] + arrived(0) + arrived(1)).astype(BF16)
            window[k, own] = v[k].astype(BF16)
            window[k, following] = (local_window[following, :] + arrived(4) + arrived(5)).astype(
                BF16
            )

    keeps = [
        pltpu.make_async_copy(v.at[k], out, keep_sem.at[k])
        for k, out in enumerate((basis0_hbm, basis1_hbm, basis2_hbm))
    ]
    send_contribs(0, picked)

    loads[7].wait()
    reach = dot(pick[...], corner[...])
    loads[9].wait()
    spread = jnp.dot(reach, stiff[...], precision=lax.Precision.HIGHEST, preferred_element_type=F32)
    for block in range(3):
        coarse[blocks[block], (2 - block) * CORNERS : (3 - block) * CORNERS] = spread[
            blocks[block]
        ].astype(BF16)

    for i in reversed(used_routes(0)):
        coarse_copy(i).start()
    high, low = two_parts(reach)
    corner_w[:, :CORNERS] = high
    corner_w[:, CORNERS:] = low
    high, low = two_parts(jnp.transpose(reach))
    corner_t[:CORNERS, :] = high
    corner_t[CORNERS:, :] = low
    place_t = as_column(place.astype(F32))

    def build_pick_t(j, carry):
        lanes = pl.ds(pl.multiple_of(j * CASES, CASES), CASES)
        at = lax.broadcasted_iota(jnp.int32, (SLOTS, CASES), 1) + j * CASES
        pick_t[:, lanes] = jnp.where(place_t == at.astype(F32), 1.0, 0.0).astype(BF16)
        return carry

    lax.fori_loop(0, SLOTS // CASES, build_pick_t, 0)
    loads[8].wait()
    receive_contribs(0)
    for k in range(2):
        both = dot(corner_t[...], window[k])
        w_part[k] = both[:CORNERS] + both[CORNERS:]
        chip_copy(k).start()
        norm = column_sum(v[k] * v[k])
        u = dot(pick_t[...], window[k]).astype(BF16)
        y = dot(dual[...], u)
        ring_sums = sum_rows(norm, column_sum(u.astype(F32) * y))
        chip_copy(k).wait_recv()
        half = w_part[k, mine] + chip_in[k]
        ring_out[k, :HALF] = half.astype(BF16)
        ring_out[k, HALF:] = ring_sums.astype(BF16)
        for copy in ring_copies(k):
            copy.start()
        high, low = two_parts(y)
        split[:, :CASES] = high
        split[:, CASES:] = low
        if k == 0:
            send_contribs(1, picked)
        else:
            for block in blocks:
                local_window[block, :] = picked(block)
        all_ring(k).wait_recv()
        for d in range(chips - 1):
            half = half + ring_in[k, d, :HALF].astype(F32)
            ring_sums = ring_sums + ring_in[k, d, HALF:].astype(F32)
        pair_out[k, :HALF] = half
        pair_out[k, HALF:] = ring_sums
        pair_copy(k).start()
        if k == 0:
            w_near[pl.ds(pl.multiple_of(2 * CORNERS + core * HALF, HALF), HALF), :] = half.astype(
                BF16
            )
            for copy in near_copies():
                copy.start()
        w_full[mine, :] = half
        pair_copy(k).wait_recv()
        w_full[theirs, :] = pair_in[k, :HALF]
        if k == 0:
            w_near[pl.ds(pl.multiple_of(3 * CORNERS - HALF - core * HALF, HALF), HALF), :] = pair_in[
                k, :HALF
            ].astype(BF16)
        ring_sums = ring_sums + pair_in[k, HALF:]
        w = w_full[...]
        z = jnp.dot(stiff[...], w, precision=lax.Precision.HIGHEST, preferred_element_type=F32)
        z_narrow = z.astype(BF16)
        z_twice = jnp.concatenate([z_narrow, z_narrow], axis=0)

        def image(rows):
            return local_window[rows, :] + dot(corner_w[rows, :], z_twice)

        if k == 1:
            send_contribs(2, image)
        energy = column_sum(w * z_narrow.astype(F32))
        totals[0, 2 * k : 2 * k + 1] = column_sum(ring_sums[0:3])
        totals[0, 2 * k + 1 : 2 * k + 2] = column_sum(ring_sums[3:6]) + energy
        if k == 1:
            send_totals()
        if k == 1:
            local_window[own, :] = image(own)
        receive_contribs(k + 1)

    all_totals().wait_recv()
    products = jnp.sum(totals[...], axis=0)
    g00, g01, g11, g12 = (products[i : i + 1] for i in range(4))
    alpha0 = g00 / g01
    norm1 = g00 - 2.0 * alpha0 * g01 + alpha0 * alpha0 * g11
    beta = norm1 / g00
    grown = 1.0 + beta
    curve = grown * grown * g01 - 2.0 * grown * alpha0 * g11 + alpha0 * alpha0 * g12
    alpha1 = norm1 / curve
    factor0[...] = alpha0 + alpha1 * grown
    factor1[...] = alpha0 * alpha1
    for copy in keeps:
        copy.wait()
    all_totals().wait_send()

    tail = near_copies() + [coarse_copy(i) for i in range(6)]
    for k in range(3):
        for i in used_routes(k):
            contrib_copy(k, i).wait_send()
    for k in range(2):
        for copy in [chip_copy(k), pair_copy(k), all_ring(k)] + (tail if k == 0 else []):
            copy.wait_send()


def solution(mesh):
    spans, subs = mesh.shape["span"], mesh.shape["sub"]
    chips = subs // 2
    vmem = pl.BlockSpec(memory_space=pltpu.VMEM)
    hbm = pl.BlockSpec(memory_space=pl.ANY)
    dma = pltpu.SemaphoreType.DMA

    def on_device(
        stress,
        history,
        retard,
        compliance,
        micro,
        lengths,
        multiplier_index,
        dual_block,
        corner_map,
        coarse_stiffness_inverse,
    ):
        units = history.shape[0]
        v0, v1, v2, first, second = pl.pallas_call(
            functools.partial(kernel, spans, subs),
            name="creep_step",
            out_shape=[jax.ShapeDtypeStruct((OWN, CASES), F32)] * 3
            + [jax.ShapeDtypeStruct((1, CASES), F32)] * 2,
            in_specs=[hbm] * 10,
            out_specs=[hbm] * 3 + [vmem] * 2,
            scratch_shapes=[
                pltpu.SMEM((units,), F32),
                pltpu.SMEM((units,), F32),
                pltpu.SMEM((1, 1), jnp.int32),
                pltpu.VMEM((SLOTS, CASES), BF16),
                pltpu.VMEM((units, 1, SLOTS), F32),
                pltpu.VMEM((1, SLOTS), F32),
                pltpu.VMEM((1, SLOTS), jnp.int32),
                pltpu.VMEM((SLOTS, SLOTS), BF16),
                pltpu.VMEM((SLOTS, CORNERS), BF16),
                pltpu.VMEM((CORNERS, CORNERS), F32),
                pltpu.VMEM((SLOTS, SLOTS), BF16),
                pltpu.VMEM((SLOTS, SLOTS), BF16),
                pltpu.VMEM((2 * CORNERS, SLOTS), BF16),
                pltpu.VMEM((SLOTS, 2 * CORNERS), BF16),
                pltpu.VMEM((SLOTS, 3 * CORNERS), BF16),
                pltpu.VMEM((5 * CORNERS, CASES), BF16),
                pltpu.VMEM((SLOTS, 2 * CASES), BF16),
                pltpu.VMEM((2, SLOTS, CASES), BF16),
                pltpu.VMEM((SLOTS, CASES), F32),
                pltpu.VMEM((3, OWN, CASES), F32),
                pltpu.VMEM((3, 3, OWN, CASES), CONTRIB),
                pltpu.VMEM((3, 6, OWN, CASES), CONTRIB),
                pltpu.VMEM((2, CORNERS, CASES), F32),
                pltpu.VMEM((CORNERS, CASES), F32),
                pltpu.VMEM((2, HALF, CASES), F32),
                pltpu.VMEM((2, HALF + SUMS, CASES), BF16),
                pltpu.VMEM((2, chips - 1, HALF + SUMS, CASES), BF16),
                pltpu.VMEM((2, HALF + SUMS, CASES), F32),
                pltpu.VMEM((2, HALF + SUMS, CASES), F32),
                pltpu.VMEM((spans, 4, CASES), F32),
                dma((10,)),
                dma((3,)),
                dma((3, 6)),
                dma((3, 6)),
                dma((6,)),
                dma((6,)),
                dma((8,)),
                dma((2,)),
                dma((2, 2)),
                dma((2, 2)),
                dma((2, 2)),
                dma((2,)),
            ],
            compiler_params=pltpu.CompilerParams(
                collective_id=0, has_side_effects=True, vmem_limit_bytes=60 * 2**20
            ),
        )(
            retard,
            compliance,
            lengths.reshape(1, 1),
            stress,
            history,
            micro,
            multiplier_index,
            dual_block,
            corner_map,
            coarse_stiffness_inverse,
        )
        return first * v0 - second * v1, v0 - first * v1 + second * v2

    rows = P(("span", "sub"), None)
    blocks = P(("span", "sub"), None, None)
    return jax.shard_map(
        on_device,
        mesh=mesh,
        in_specs=(
            blocks,
            P(None, ("span", "sub"), None),
            P(),
            P(),
            rows,
            P(("span", "sub")),
            rows,
            blocks,
            blocks,
            P("span", None, None),
        ),
        out_specs=(rows, rows),
        check_vma=False,
    )
```

```python
import functools

import jax
import jax.numpy as jnp
from jax import lax
from jax.experimental import pallas as pl
from jax.experimental.pallas import tpu as pltpu
from jax.sharding import PartitionSpec as P

MESH = pl.DeviceIdType.MESH
F32 = jnp.float32
BF16 = jnp.bfloat16
CONTRIB = jnp.bfloat16
OWN = 256
SLOTS = 768
CASES = 128
CORNERS = 128
HALF = CORNERS // 2
SUMS = 16
ROWS = 64


def dot(a, b):
    return jnp.dot(a, b, preferred_element_type=F32)


def two_parts(x):
    high = x.astype(BF16)
    return high, (x - high.astype(F32)).astype(BF16)


def column_sum(x):
    return jnp.sum(x, axis=0, keepdims=True)


def as_column(row):
    return jnp.transpose(jnp.broadcast_to(row, (CASES, SLOTS)))


def sum_rows(first, second):
    row = lax.broadcasted_iota(jnp.int32, (SUMS, CASES), 0)
    out = jnp.zeros((SUMS, CASES), F32)
    for base, value in ((0, first), (3, second)):
        rest = value
        for i in range(3):
            part = rest.astype(BF16).astype(F32)
            rest = rest - part
            out = jnp.where(row == base + i, part, out)
    return out


def kernel(
    spans,
    subs,
    retard_hbm,
    compliance_hbm,
    lengths_hbm,
    stress_hbm,
    history_hbm,
    micro_hbm,
    index_hbm,
    dual_hbm,
    corner_hbm,
    stiff_hbm,
    basis0,
    basis1,
    basis2,
    factor0,
    factor1,
    retard,
    compliance,
    lengths,
    stress,
    history,
    micro,
    index,
    dual,
    corner,
    stiff,
    pick,
    pick_t,
    corner_t,
    corner_w,
    coarse,
    w_near,
    split,
    window,
    local_window,
    contrib_out,
    contrib_in,
    w_part,
    w_full,
    chip_in,
    ring_out,
    ring_in,
    pair_out,
    pair_in,
    totals,
    load_sem,
    contrib_send,
    contrib_recv,
    coarse_send,
    coarse_recv,
    near_send,
    near_recv,
    chip_sem,
    ring_sem,
    pair_sem,
    total_sem,
):
    basis = (basis0, basis1, basis2)
    p = lax.axis_index("span")
    s = lax.axis_index("sub")
    chips = subs // 2
    core = lax.rem(s, 2)
    partner = (p, s + 1 - 2 * core)
    mine = pl.ds(pl.multiple_of(core * HALF, HALF), HALF)
    theirs = pl.ds(pl.multiple_of((1 - core) * HALF, HALF), HALF)

    loads = [
        pltpu.make_async_copy(src, dst, load_sem.at[i])
        for i, (src, dst) in enumerate(
            (
                (lengths_hbm, lengths),
                (index_hbm, index),
                (retard_hbm, retard),
                (compliance_hbm, compliance),
                (micro_hbm, micro),
                (history_hbm, history),
                (stress_hbm.at[0], stress),
                (corner_hbm.at[0], corner),
                (dual_hbm.at[0], dual),
                (stiff_hbm.at[0], stiff),
            )
        )
    ]
    for copy in loads:
        copy.start()

    barrier = pltpu.get_barrier_semaphore()

    def greet_span(d, carry):
        pl.semaphore_signal(
            barrier, inc=1, device_id=(lax.rem(p + d, spans), s), device_id_type=MESH
        )
        return carry

    def greet_chip(d, carry):
        pl.semaphore_signal(
            barrier, inc=1, device_id=(p, lax.rem(s + 2 * d, subs)), device_id_type=MESH
        )
        return carry

    pl.semaphore_signal(barrier, inc=1, device_id=partner, device_id_type=MESH)
    for d in (1, spans - 1, 2, spans - 2):
        greet_span(d, 0)
        pl.semaphore_signal(
            barrier, inc=1, device_id=(lax.rem(p + d, spans), partner[1]), device_id_type=MESH
        )
    lax.fori_loop(1, chips, greet_chip, 0)
    lax.fori_loop(3, spans - 2, greet_span, 0)

    loads[0].wait()
    loads[1].wait()
    slot = lax.broadcasted_iota(jnp.int32, (1, SLOTS), 1)
    owner_span = index[...] // (OWN * subs)
    place = (owner_span - p + 1) * OWN + lax.rem(index[...], OWN)
    place = jnp.where(slot < lengths[0, 0], place, -1)

    def build_pick(i, carry):
        rows = pl.ds(pl.multiple_of(i * ROWS, ROWS), ROWS)
        at = lax.broadcasted_iota(jnp.int32, (ROWS, SLOTS), 0) + i * ROWS
        pick[rows, :] = jnp.where(at == place, 1.0, 0.0).astype(BF16)
        return carry

    lax.fori_loop(0, SLOTS // ROWS, build_pick, 0)

    for copy in loads[2:6]:
        copy.wait()
    creep = jnp.zeros((1, SLOTS), F32)
    past = jnp.zeros((1, SLOTS), F32)
    for k in range(history.shape[0]):
        weight = 1.0 - jnp.exp(-1.0 / jnp.full((1, SLOTS), retard[k], F32))
        creep = creep + weight * compliance[k]
        past = past + weight * history[k]
    relaxed = micro[...] / (1.0 + micro[...])
    scale = as_column(creep + 0.5 * relaxed)
    past = as_column(past)
    loads[6].wait()
    load = scale * stress[...].astype(F32) - past
    high, low = two_parts(load)
    split[:, :CASES] = high
    split[:, CASES:] = low

    def picked(rows):
        both = dot(pick[rows, :], split[...])
        return both[:, :CASES] + both[:, CASES:]

    routes = ((1, 1), (2, 2), (2, 1), (0, -1), (1, -1), (0, -2))

    def contrib_copy(k, i):
        block, onward = routes[i]
        return pltpu.make_async_remote_copy(
            src_ref=contrib_out.at[k, block],
            dst_ref=contrib_in.at[k, i],
            send_sem=contrib_send.at[k, i],
            recv_sem=contrib_recv.at[k, i],
            device_id=(lax.rem(p + spans + onward, spans), s),
            device_id_type=MESH,
        )

    landing = ((0, 1), (0, 0), (1, 0), (1, 2), (2, 1), (2, 2))

    def coarse_copy(i):
        block, onward = routes[i]
        row, column = landing[i]
        return pltpu.make_async_remote_copy(
            src_ref=coarse.at[pl.ds(block * OWN, OWN), pl.ds((2 - block) * CORNERS, CORNERS)],
            dst_ref=coarse.at[pl.ds(row * OWN, OWN), pl.ds(column * CORNERS, CORNERS)],
            send_sem=coarse_send.at[i],
            recv_sem=coarse_recv.at[i],
            device_id=(lax.rem(p + spans + onward, spans), s),
            device_id_type=MESH,
        )

    def near_copies():
        kept = w_near.at[pl.ds(pl.multiple_of(2 * CORNERS + core * HALF, HALF), HALF)]
        copies = []
        for onward in (2, -2, 1, -1):
            place = pl.multiple_of((2 - onward) * CORNERS + core * HALF, HALF)
            for to in (s, partner[1]):
                copies.append(
                    pltpu.make_async_remote_copy(
                        src_ref=kept,
                        dst_ref=w_near.at[pl.ds(place, HALF)],
                        send_sem=near_send.at[len(copies)],
                        recv_sem=near_recv.at[0 if onward > 0 else 1],
                        device_id=(lax.rem(p + spans + onward, spans), to),
                        device_id_type=MESH,
                    )
                )
        return copies

    def all_near(side):
        rows = w_near.at[pl.ds(side * 3 * CORNERS, 2 * CORNERS)]
        return pltpu.make_async_remote_copy(
            src_ref=rows,
            dst_ref=rows,
            send_sem=near_send.at[0],
            recv_sem=near_recv.at[side],
            device_id=partner,
            device_id_type=MESH,
        )

    def used_routes(k):
        return range(6) if k < 2 else (2, 3)

    def chip_copy(k):
        return pltpu.make_async_remote_copy(
            src_ref=w_part.at[k, theirs],
            dst_ref=chip_in.at[k],
            send_sem=chip_sem.at[k, 0],
            recv_sem=chip_sem.at[k, 1],
            device_id=partner,
            device_id_type=MESH,
        )

    def ring_copies(k):
        return [
            pltpu.make_async_remote_copy(
                src_ref=ring_out.at[k],
                dst_ref=ring_in.at[k, d - 1],
                send_sem=ring_sem.at[k, 0],
                recv_sem=ring_sem.at[k, 1],
                device_id=(p, lax.rem(s + 2 * d, subs)),
                device_id_type=MESH,
            )
            for d in sorted(range(1, chips), key=lambda d: -min(d, chips - d))
        ]

    def all_ring(k):
        return pltpu.make_async_remote_copy(
            src_ref=ring_in.at[k],
            dst_ref=ring_in.at[k],
            send_sem=ring_sem.at[k, 0],
            recv_sem=ring_sem.at[k, 1],
            device_id=partner,
            device_id_type=MESH,
        )

    def pair_copy(k):
        return pltpu.make_async_remote_copy(
            src_ref=pair_out.at[k],
            dst_ref=pair_in.at[k],
            send_sem=pair_sem.at[k, 0],
            recv_sem=pair_sem.at[k, 1],
            device_id=partner,
            device_id_type=MESH,
        )

    def send_totals():
        def step(i, carry):
            d = 1 + lax.rem(i + spans // 3, spans - 1)
            pltpu.make_async_remote_copy(
                src_ref=totals.at[0],
                dst_ref=totals.at[d],
                send_sem=total_sem.at[0],
                recv_sem=total_sem.at[1],
                device_id=(lax.rem(p + d, spans), s),
                device_id_type=MESH,
            ).start()
            return carry

        lax.fori_loop(0, spans - 1, step, 0)

    def all_totals():
        rest = totals.at[pl.ds(1, spans - 1)]
        return pltpu.make_async_remote_copy(
            src_ref=rest,
            dst_ref=rest,
            send_sem=total_sem.at[0],
            recv_sem=total_sem.at[1],
            device_id=partner,
            device_id_type=MESH,
        )

    previous, own, following = blocks = [slice(i * OWN, (i + 1) * OWN) for i in range(3)]

    def send_contribs(k, image):
        for block in (0, 2, 1) if k < 2 else (0, 2):
            value = image(blocks[block])
            if k < 2:
                local_window[blocks[block], :] = value
            contrib_out[k, block] = value.astype(CONTRIB)
            if k == 0 and block == 0:
                pl.semaphore_wait(barrier, spans + chips + 3)
            for i in sorted(used_routes(k), key=lambda i: -abs(routes[i][1])):
                if routes[i][0] == block:
                    contrib_copy(k, i).start()

    def receive_contribs(k):
        for i in used_routes(k):
            contrib_copy(k, i).wait_recv()

        def arrived(i):
            return contrib_in[k, i].astype(F32)

        if k == 1:
            for i in used_routes(k):
                coarse_copy(i).wait_recv()
            for side in range(2):
                all_near(side).wait_recv()
            for block in range(3):
                near = w_near[block * CORNERS : (block + 3) * CORNERS, :]
                local_window[blocks[block], :] += dot(coarse[blocks[block], :], near)
        basis[k][...] = local_window[own, :] + arrived(2) + arrived(3)
        if k < 2:
            window[k, previous] = (local_window[previous, :] + arrived(0) + arrived(1)).astype(BF16)
            window[k, own] = basis[k][...].astype(BF16)
            window[k, following] = (local_window[following, :] + arrived(4) + arrived(5)).astype(
                BF16
            )

    send_contribs(0, picked)

    loads[7].wait()
    reach = dot(pick[...], corner[...])
    loads[9].wait()
    spread = jnp.dot(reach, stiff[...], precision=lax.Precision.HIGHEST, preferred_element_type=F32)
    for block in range(3):
        coarse[blocks[block], (2 - block) * CORNERS : (3 - block) * CORNERS] = spread[
            blocks[block]
        ].astype(BF16)

    high, low = two_parts(reach)
    corner_w[:, :CORNERS] = high
    corner_w[:, CORNERS:] = low
    high, low = two_parts(jnp.transpose(reach))
    corner_t[:CORNERS, :] = high
    corner_t[CORNERS:, :] = low
    place_t = as_column(place.astype(F32))

    def build_pick_t(j, carry):
        lanes = pl.ds(pl.multiple_of(j * CASES, CASES), CASES)
        at = lax.broadcasted_iota(jnp.int32, (SLOTS, CASES), 1) + j * CASES
        pick_t[:, lanes] = jnp.where(place_t == at.astype(F32), 1.0, 0.0).astype(BF16)
        return carry

    lax.fori_loop(0, SLOTS // CASES, build_pick_t, 0)
    loads[8].wait()
    for i in used_routes(0):
        contrib_copy(0, i).wait_send()
    for i in reversed(used_routes(0)):
        coarse_copy(i).start()
    receive_contribs(0)
    for k in range(2):
        both = dot(corner_t[...], window[k])
        w_part[k] = both[:CORNERS] + both[CORNERS:]
        chip_copy(k).start()
        norm = column_sum(basis[k][...] * basis[k][...])
        u = dot(pick_t[...], window[k]).astype(BF16)
        y = dot(dual[...], u)
        ring_sums = sum_rows(norm, column_sum(u.astype(F32) * y))
        chip_copy(k).wait_recv()
        half = w_part[k, mine] + chip_in[k]
        ring_out[k, :HALF] = half.astype(BF16)
        ring_out[k, HALF:] = ring_sums.astype(BF16)
        for copy in ring_copies(k):
            copy.start()
        high, low = two_parts(y)
        split[:, :CASES] = high
        split[:, CASES:] = low
        if k == 0:
            send_contribs(1, picked)
        else:
            for block in blocks:
                local_window[block, :] = picked(block)
        all_ring(k).wait_recv()
        for d in range(chips - 1):
            half = half + ring_in[k, d, :HALF].astype(F32)
            ring_sums = ring_sums + ring_in[k, d, HALF:].astype(F32)
        pair_out[k, :HALF] = half
        pair_out[k, HALF:] = ring_sums
        pair_copy(k).start()
        if k == 0:
            w_near[pl.ds(pl.multiple_of(2 * CORNERS + core * HALF, HALF), HALF), :] = half.astype(
                BF16
            )
            for copy in near_copies():
                copy.start()
        w_full[mine, :] = half
        pair_copy(k).wait_recv()
        w_full[theirs, :] = pair_in[k, :HALF]
        if k == 0:
            w_near[pl.ds(pl.multiple_of(3 * CORNERS - HALF - core * HALF, HALF), HALF), :] = pair_in[
                k, :HALF
            ].astype(BF16)
        ring_sums = ring_sums + pair_in[k, HALF:]
        w = w_full[...]
        z = jnp.dot(stiff[...], w, precision=lax.Precision.HIGHEST, preferred_element_type=F32)
        z_narrow = z.astype(BF16)
        z_twice = jnp.concatenate([z_narrow, z_narrow], axis=0)

        def image(rows):
            return local_window[rows, :] + dot(corner_w[rows, :], z_twice)

        if k == 1:
            send_contribs(2, image)
        energy = column_sum(w * z_narrow.astype(F32))
        totals[0, 2 * k : 2 * k + 1] = column_sum(ring_sums[0:3])
        totals[0, 2 * k + 1 : 2 * k + 2] = column_sum(ring_sums[3:6]) + energy
        if k == 1:
            send_totals()
        if k == 1:
            local_window[own, :] = image(own)
        receive_contribs(k + 1)

    all_totals().wait_recv()
    products = jnp.sum(totals[...], axis=0)
    g00, g01, g11, g12 = (products[i : i + 1] for i in range(4))
    alpha0 = g00 / g01
    norm1 = g00 - 2.0 * alpha0 * g01 + alpha0 * alpha0 * g11
    beta = norm1 / g00
    grown = 1.0 + beta
    curve = grown * grown * g01 - 2.0 * grown * alpha0 * g11 + alpha0 * alpha0 * g12
    alpha1 = norm1 / curve
    factor0[...] = alpha0 + alpha1 * grown
    factor1[...] = alpha0 * alpha1
    all_totals().wait_send()

    tail = near_copies() + [coarse_copy(i) for i in range(6)]
    for k in range(1, 3):
        for i in used_routes(k):
            contrib_copy(k, i).wait_send()
    for k in range(2):
        for copy in [chip_copy(k), pair_copy(k), all_ring(k)] + (tail if k == 0 else []):
            copy.wait_send()


def solution(mesh):
    spans, subs = mesh.shape["span"], mesh.shape["sub"]
    chips = subs // 2
    vmem = pl.BlockSpec(memory_space=pltpu.VMEM)
    hbm = pl.BlockSpec(memory_space=pl.ANY)
    dma = pltpu.SemaphoreType.DMA

    def on_device(
        stress,
        history,
        retard,
        compliance,
        micro,
        lengths,
        multiplier_index,
        dual_block,
        corner_map,
        coarse_stiffness_inverse,
    ):
        units = history.shape[0]
        v0, v1, v2, first, second = pl.pallas_call(
            functools.partial(kernel, spans, subs),
            name="creep_step",
            out_shape=[pltpu.VMEM((OWN, CASES), F32)] * 3
            + [pltpu.VMEM((1, CASES), F32)] * 2,
            in_specs=[hbm] * 10,
            out_specs=[vmem] * 5,
            scratch_shapes=[
                pltpu.SMEM((units,), F32),
                pltpu.SMEM((units,), F32),
                pltpu.SMEM((1, 1), jnp.int32),
                pltpu.VMEM((SLOTS, CASES), BF16),
                pltpu.VMEM((units, 1, SLOTS), F32),
                pltpu.VMEM((1, SLOTS), F32),
                pltpu.VMEM((1, SLOTS), jnp.int32),
                pltpu.VMEM((SLOTS, SLOTS), BF16),
                pltpu.VMEM((SLOTS, CORNERS), BF16),
                pltpu.VMEM((CORNERS, CORNERS), F32),
                pltpu.VMEM((SLOTS, SLOTS), BF16),
                pltpu.VMEM((SLOTS, SLOTS), BF16),
                pltpu.VMEM((2 * CORNERS, SLOTS), BF16),
                pltpu.VMEM((SLOTS, 2 * CORNERS), BF16),
                pltpu.VMEM((SLOTS, 3 * CORNERS), BF16),
                pltpu.VMEM((5 * CORNERS, CASES), BF16),
                pltpu.VMEM((SLOTS, 2 * CASES), BF16),
                pltpu.VMEM((2, SLOTS, CASES), BF16),
                pltpu.VMEM((SLOTS, CASES), F32),
                pltpu.VMEM((3, 3, OWN, CASES), CONTRIB),
                pltpu.VMEM((3, 6, OWN, CASES), CONTRIB),
                pltpu.VMEM((2, CORNERS, CASES), F32),
                pltpu.VMEM((CORNERS, CASES), F32),
                pltpu.VMEM((2, HALF, CASES), F32),
                pltpu.VMEM((2, HALF + SUMS, CASES), BF16),
                pltpu.VMEM((2, chips - 1, HALF + SUMS, CASES), BF16),
                pltpu.VMEM((2, HALF + SUMS, CASES), F32),
                pltpu.VMEM((2, HALF + SUMS, CASES), F32),
                pltpu.VMEM((spans, 4, CASES), F32),
                dma((10,)),
                dma((3, 6)),
                dma((3, 6)),
                dma((6,)),
                dma((6,)),
                dma((8,)),
                dma((2,)),
                dma((2, 2)),
                dma((2, 2)),
                dma((2, 2)),
                dma((2,)),
            ],
            compiler_params=pltpu.CompilerParams(
                collective_id=0, has_side_effects=True, vmem_limit_bytes=60 * 2**20
            ),
        )(
            retard,
            compliance,
            lengths.reshape(1, 1),
            stress,
            history,
            micro,
            multiplier_index,
            dual_block,
            corner_map,
            coarse_stiffness_inverse,
        )
        return first * v0 - second * v1, v0 - first * v1 + second * v2

    rows = P(("span", "sub"), None)
    blocks = P(("span", "sub"), None, None)
    return jax.shard_map(
        on_device,
        mesh=mesh,
        in_specs=(
            blocks,
            P(None, ("span", "sub"), None),
            P(),
            P(),
            rows,
            P(("span", "sub")),
            rows,
            blocks,
            blocks,
            P("span", None, None),
        ),
        out_specs=(rows, rows),
        check_vma=False,
    )
```

```python
import functools

import jax
import jax.numpy as jnp
from jax import lax
from jax.experimental import pallas as pl
from jax.experimental.pallas import tpu as pltpu
from jax.sharding import PartitionSpec as P

MESH = pl.DeviceIdType.MESH
F32 = jnp.float32
BF16 = jnp.bfloat16
CONTRIB = jnp.bfloat16
OWN = 256
SLOTS = 768
CASES = 128
CORNERS = 128
HALF = CORNERS // 2
SUMS = 16
ROWS = 64


def dot(a, b):
    return jnp.dot(a, b, preferred_element_type=F32)


def two_parts(x):
    high = x.astype(BF16)
    return high, (x - high.astype(F32)).astype(BF16)


def column_sum(x):
    return jnp.sum(x, axis=0, keepdims=True)


def as_column(row):
    return jnp.transpose(jnp.broadcast_to(row, (CASES, SLOTS)))


def sum_rows(values):
    row = lax.broadcasted_iota(jnp.int32, (SUMS, CASES), 0)
    out = jnp.zeros((SUMS, CASES), F32)
    for number, value in enumerate(values):
        base, rest = 3 * number, value
        for i in range(3):
            part = rest.astype(BF16).astype(F32)
            rest = rest - part
            out = jnp.where(row == base + i, part, out)
    return out


def kernel(
    spans,
    subs,
    retard_hbm,
    compliance_hbm,
    lengths_hbm,
    stress_hbm,
    history_hbm,
    micro_hbm,
    index_hbm,
    dual_hbm,
    corner_hbm,
    stiff_hbm,
    basis0,
    basis1,
    basis2,
    factor0,
    factor1,
    retard,
    compliance,
    lengths,
    stress,
    history,
    micro,
    index,
    dual,
    corner,
    stiff,
    pick,
    pick_t,
    corner_t,
    corner_w,
    coarse,
    w_near,
    split,
    window,
    local_window,
    contrib_out,
    contrib_in,
    w_part,
    w_full,
    chip_in,
    ring_out,
    ring_in,
    pair_out,
    pair_in,
    totals,
    load_sem,
    contrib_send,
    contrib_recv,
    coarse_send,
    coarse_recv,
    near_send,
    near_recv,
    chip_sem,
    ring_sem,
    pair_sem,
    total_sem,
):
    basis = (basis0, basis1, basis2)
    p = lax.axis_index("span")
    s = lax.axis_index("sub")
    chips = subs // 2
    core = lax.rem(s, 2)
    partner = (p, s + 1 - 2 * core)
    mine = pl.ds(pl.multiple_of(core * HALF, HALF), HALF)
    theirs = pl.ds(pl.multiple_of((1 - core) * HALF, HALF), HALF)

    loads = [
        pltpu.make_async_copy(src, dst, load_sem.at[i])
        for i, (src, dst) in enumerate(
            (
                (lengths_hbm, lengths),
                (index_hbm, index),
                (retard_hbm, retard),
                (compliance_hbm, compliance),
                (micro_hbm, micro),
                (history_hbm, history),
                (stress_hbm.at[0], stress),
                (corner_hbm.at[0], corner),
                (dual_hbm.at[0], dual),
                (stiff_hbm.at[0], stiff),
            )
        )
    ]
    for copy in loads:
        copy.start()

    barrier = pltpu.get_barrier_semaphore()

    def greet_span(d, carry):
        pl.semaphore_signal(
            barrier, inc=1, device_id=(lax.rem(p + d, spans), s), device_id_type=MESH
        )
        return carry

    def greet_chip(d, carry):
        pl.semaphore_signal(
            barrier, inc=1, device_id=(p, lax.rem(s + 2 * d, subs)), device_id_type=MESH
        )
        return carry

    pl.semaphore_signal(barrier, inc=1, device_id=partner, device_id_type=MESH)
    for d in (1, spans - 1, 2, spans - 2):
        greet_span(d, 0)
        pl.semaphore_signal(
            barrier, inc=1, device_id=(lax.rem(p + d, spans), partner[1]), device_id_type=MESH
        )
    lax.fori_loop(1, chips, greet_chip, 0)
    lax.fori_loop(3, spans - 2, greet_span, 0)

    loads[0].wait()
    loads[1].wait()
    slot = lax.broadcasted_iota(jnp.int32, (1, SLOTS), 1)
    owner_span = index[...] // (OWN * subs)
    place = (owner_span - p + 1) * OWN + lax.rem(index[...], OWN)
    place = jnp.where(slot < lengths[0, 0], place, -1)

    def build_pick(i, carry):
        rows = pl.ds(pl.multiple_of(i * ROWS, ROWS), ROWS)
        at = lax.broadcasted_iota(jnp.int32, (ROWS, SLOTS), 0) + i * ROWS
        pick[rows, :] = jnp.where(at == place, 1.0, 0.0).astype(BF16)
        return carry

    lax.fori_loop(0, SLOTS // ROWS, build_pick, 0)

    for copy in loads[2:6]:
        copy.wait()
    creep = jnp.zeros((1, SLOTS), F32)
    past = jnp.zeros((1, SLOTS), F32)
    for k in range(history.shape[0]):
        weight = 1.0 - jnp.exp(-1.0 / jnp.full((1, SLOTS), retard[k], F32))
        creep = creep + weight * compliance[k]
        past = past + weight * history[k]
    relaxed = micro[...] / (1.0 + micro[...])
    scale = as_column(creep + 0.5 * relaxed)
    past = as_column(past)
    loads[6].wait()
    load = scale * stress[...].astype(F32) - past
    high, low = two_parts(load)
    split[:, :CASES] = high
    split[:, CASES:] = low

    def picked(rows):
        both = dot(pick[rows, :], split[...])
        return both[:, :CASES] + both[:, CASES:]

    routes = ((1, 1), (2, 2), (2, 1), (0, -1), (1, -1), (0, -2))

    def contrib_copy(k, i):
        block, onward = routes[i]
        return pltpu.make_async_remote_copy(
            src_ref=contrib_out.at[k, block],
            dst_ref=contrib_in.at[k, i],
            send_sem=contrib_send.at[k, i],
            recv_sem=contrib_recv.at[k, i],
            device_id=(lax.rem(p + spans + onward, spans), s),
            device_id_type=MESH,
        )

    landing = ((0, 1), (0, 0), (1, 0), (1, 2), (2, 1), (2, 2))

    def coarse_copy(i):
        block, onward = routes[i]
        row, column = landing[i]
        return pltpu.make_async_remote_copy(
            src_ref=coarse.at[pl.ds(block * OWN, OWN), pl.ds((2 - block) * CORNERS, CORNERS)],
            dst_ref=coarse.at[pl.ds(row * OWN, OWN), pl.ds(column * CORNERS, CORNERS)],
            send_sem=coarse_send.at[i],
            recv_sem=coarse_recv.at[i],
            device_id=(lax.rem(p + spans + onward, spans), s),
            device_id_type=MESH,
        )

    def near_copies():
        kept = w_near.at[pl.ds(pl.multiple_of(2 * CORNERS + core * HALF, HALF), HALF)]
        copies = []
        for onward in (2, -2, 1, -1):
            place = pl.multiple_of((2 - onward) * CORNERS + core * HALF, HALF)
            for to in (s, partner[1]):
                copies.append(
                    pltpu.make_async_remote_copy(
                        src_ref=kept,
                        dst_ref=w_near.at[pl.ds(place, HALF)],
                        send_sem=near_send.at[len(copies)],
                        recv_sem=near_recv.at[0 if onward > 0 else 1],
                        device_id=(lax.rem(p + spans + onward, spans), to),
                        device_id_type=MESH,
                    )
                )
        return copies

    def all_near(side):
        rows = w_near.at[pl.ds(side * 3 * CORNERS, 2 * CORNERS)]
        return pltpu.make_async_remote_copy(
            src_ref=rows,
            dst_ref=rows,
            send_sem=near_send.at[0],
            recv_sem=near_recv.at[side],
            device_id=partner,
            device_id_type=MESH,
        )

    def used_routes(k):
        return range(6) if k < 2 else (2, 3)

    def chip_copy(k):
        return pltpu.make_async_remote_copy(
            src_ref=w_part.at[k, theirs],
            dst_ref=chip_in.at[k],
            send_sem=chip_sem.at[k, 0],
            recv_sem=chip_sem.at[k, 1],
            device_id=partner,
            device_id_type=MESH,
        )

    ring_rows = (HALF, HALF + SUMS)

    def ring_copies(k):
        return [
            pltpu.make_async_remote_copy(
                src_ref=ring_out.at[k, pl.ds(0, ring_rows[k])],
                dst_ref=ring_in.at[k, d - 1, pl.ds(0, ring_rows[k])],
                send_sem=ring_sem.at[k, 0],
                recv_sem=ring_sem.at[k, 1],
                device_id=(p, lax.rem(s + 2 * d, subs)),
                device_id_type=MESH,
            )
            for d in sorted(range(1, chips), key=lambda d: -min(d, chips - d))
        ]

    def all_ring(k):
        return pltpu.make_async_remote_copy(
            src_ref=ring_in.at[k, :, pl.ds(0, ring_rows[k])],
            dst_ref=ring_in.at[k, :, pl.ds(0, ring_rows[k])],
            send_sem=ring_sem.at[k, 0],
            recv_sem=ring_sem.at[k, 1],
            device_id=partner,
            device_id_type=MESH,
        )

    def pair_copy(k):
        return pltpu.make_async_remote_copy(
            src_ref=pair_out.at[k, pl.ds(0, ring_rows[k])],
            dst_ref=pair_in.at[k, pl.ds(0, ring_rows[k])],
            send_sem=pair_sem.at[k, 0],
            recv_sem=pair_sem.at[k, 1],
            device_id=partner,
            device_id_type=MESH,
        )

    def send_totals():
        def step(i, carry):
            d = 1 + lax.rem(i + spans // 3, spans - 1)
            pltpu.make_async_remote_copy(
                src_ref=totals.at[0],
                dst_ref=totals.at[d],
                send_sem=total_sem.at[0],
                recv_sem=total_sem.at[1],
                device_id=(lax.rem(p + d, spans), s),
                device_id_type=MESH,
            ).start()
            return carry

        lax.fori_loop(0, spans - 1, step, 0)

    def all_totals():
        rest = totals.at[pl.ds(1, spans - 1)]
        return pltpu.make_async_remote_copy(
            src_ref=rest,
            dst_ref=rest,
            send_sem=total_sem.at[0],
            recv_sem=total_sem.at[1],
            device_id=partner,
            device_id_type=MESH,
        )

    previous, own, following = blocks = [slice(i * OWN, (i + 1) * OWN) for i in range(3)]

    def send_contribs(k, image):
        for block in (0, 2, 1) if k < 2 else (0, 2):
            value = image(blocks[block])
            if k < 2:
                local_window[blocks[block], :] = value
            contrib_out[k, block] = value.astype(CONTRIB)
            if k == 0 and block == 0:
                pl.semaphore_wait(barrier, spans + chips + 3)
            for i in sorted(used_routes(k), key=lambda i: -abs(routes[i][1])):
                if routes[i][0] == block:
                    contrib_copy(k, i).start()

    def receive_contribs(k):
        for i in used_routes(k):
            contrib_copy(k, i).wait_recv()

        def arrived(i):
            return contrib_in[k, i].astype(F32)

        if k == 1:
            for i in used_routes(k):
                coarse_copy(i).wait_recv()
            for side in range(2):
                all_near(side).wait_recv()
            for block in range(3):
                near = w_near[block * CORNERS : (block + 3) * CORNERS, :]
                local_window[blocks[block], :] += dot(coarse[blocks[block], :], near)
        basis[k][...] = local_window[own, :] + arrived(2) + arrived(3)
        if k < 2:
            window[k, previous] = (local_window[previous, :] + arrived(0) + arrived(1)).astype(BF16)
            window[k, own] = basis[k][...].astype(BF16)
            window[k, following] = (local_window[following, :] + arrived(4) + arrived(5)).astype(
                BF16
            )

    send_contribs(0, picked)

    loads[7].wait()
    reach = dot(pick[...], corner[...])
    loads[9].wait()
    spread = jnp.dot(reach, stiff[...], precision=lax.Precision.HIGHEST, preferred_element_type=F32)
    for block in range(3):
        coarse[blocks[block], (2 - block) * CORNERS : (3 - block) * CORNERS] = spread[
            blocks[block]
        ].astype(BF16)

    high, low = two_parts(reach)
    corner_w[:, :CORNERS] = high
    corner_w[:, CORNERS:] = low
    high, low = two_parts(jnp.transpose(reach))
    corner_t[:CORNERS, :] = high
    corner_t[CORNERS:, :] = low
    place_t = as_column(place.astype(F32))

    def build_pick_t(j, carry):
        lanes = pl.ds(pl.multiple_of(j * CASES, CASES), CASES)
        at = lax.broadcasted_iota(jnp.int32, (SLOTS, CASES), 1) + j * CASES
        pick_t[:, lanes] = jnp.where(place_t == at.astype(F32), 1.0, 0.0).astype(BF16)
        return carry

    lax.fori_loop(0, SLOTS // CASES, build_pick_t, 0)
    loads[8].wait()
    for i in used_routes(0):
        contrib_copy(0, i).wait_send()
    for i in reversed(used_routes(0)):
        coarse_copy(i).start()
    receive_contribs(0)
    products_so_far, energies = [], []
    for k in range(2):
        both = dot(corner_t[...], window[k])
        w_part[k] = both[:CORNERS] + both[CORNERS:]
        chip_copy(k).start()
        u = dot(pick_t[...], window[k]).astype(BF16)

        def products():
            products_so_far.append(column_sum(basis[k][...] * basis[k][...]))
            y = dot(dual[...], u)
            products_so_far.append(column_sum(u.astype(F32) * y))
            return y

        if k == 1:
            y = products()
            ring_sums = sum_rows(products_so_far)
            ring_out[k, HALF:] = ring_sums.astype(BF16)
        chip_copy(k).wait_recv()
        half = w_part[k, mine] + chip_in[k]
        ring_out[k, :HALF] = half.astype(BF16)
        for copy in ring_copies(k):
            copy.start()
        if k == 0:
            y = products()
        high, low = two_parts(y)
        split[:, :CASES] = high
        split[:, CASES:] = low
        if k == 0:
            send_contribs(1, picked)
        else:
            for block in blocks:
                local_window[block, :] = picked(block)
        all_ring(k).wait_recv()
        for d in range(chips - 1):
            half = half + ring_in[k, d, :HALF].astype(F32)
            if k == 1:
                ring_sums = ring_sums + ring_in[k, d, HALF:].astype(F32)
        pair_out[k, :HALF] = half
        if k == 1:
            pair_out[k, HALF:] = ring_sums
        pair_copy(k).start()
        if k == 0:
            w_near[pl.ds(pl.multiple_of(2 * CORNERS + core * HALF, HALF), HALF), :] = half.astype(
                BF16
            )
            for copy in near_copies():
                copy.start()
        w_full[mine, :] = half
        pair_copy(k).wait_recv()
        w_full[theirs, :] = pair_in[k, :HALF]
        if k == 0:
            w_near[pl.ds(pl.multiple_of(3 * CORNERS - HALF - core * HALF, HALF), HALF), :] = pair_in[
                k, :HALF
            ].astype(BF16)
        w = w_full[...]
        z = jnp.dot(stiff[...], w, precision=lax.Precision.HIGHEST, preferred_element_type=F32)
        z_narrow = z.astype(BF16)
        z_twice = jnp.concatenate([z_narrow, z_narrow], axis=0)

        def image(rows):
            return local_window[rows, :] + dot(corner_w[rows, :], z_twice)

        energies.append(column_sum(w * z_narrow.astype(F32)))
        if k == 1:
            ring_sums = ring_sums + pair_in[k, HALF:]
            for i in range(4):
                row = column_sum(ring_sums[3 * i : 3 * i + 3])
                totals[0, i : i + 1] = row + energies[i // 2] if i % 2 else row
            send_totals()
            send_contribs(2, image)
        if k == 1:
            local_window[own, :] = image(own)
        receive_contribs(k + 1)

    all_totals().wait_recv()
    products = jnp.sum(totals[...], axis=0)
    g00, g01, g11, g12 = (products[i : i + 1] for i in range(4))
    alpha0 = g00 / g01
    norm1 = g00 - 2.0 * alpha0 * g01 + alpha0 * alpha0 * g11
    beta = norm1 / g00
    grown = 1.0 + beta
    curve = grown * grown * g01 - 2.0 * grown * alpha0 * g11 + alpha0 * alpha0 * g12
    alpha1 = norm1 / curve
    factor0[...] = alpha0 + alpha1 * grown
    factor1[...] = alpha0 * alpha1
    all_totals().wait_send()

    tail = near_copies() + [coarse_copy(i) for i in range(6)]
    for k in range(1, 3):
        for i in used_routes(k):
            contrib_copy(k, i).wait_send()
    for k in range(2):
        for copy in [chip_copy(k), pair_copy(k), all_ring(k)] + (tail if k == 0 else []):
            copy.wait_send()


def solution(mesh):
    spans, subs = mesh.shape["span"], mesh.shape["sub"]
    chips = subs // 2
    vmem = pl.BlockSpec(memory_space=pltpu.VMEM)
    hbm = pl.BlockSpec(memory_space=pl.ANY)
    dma = pltpu.SemaphoreType.DMA

    def on_device(
        stress,
        history,
        retard,
        compliance,
        micro,
        lengths,
        multiplier_index,
        dual_block,
        corner_map,
        coarse_stiffness_inverse,
    ):
        units = history.shape[0]
        v0, v1, v2, first, second = pl.pallas_call(
            functools.partial(kernel, spans, subs),
            name="creep_step",
            out_shape=[pltpu.VMEM((OWN, CASES), F32)] * 3
            + [pltpu.VMEM((1, CASES), F32)] * 2,
            in_specs=[hbm] * 10,
            out_specs=[vmem] * 5,
            scratch_shapes=[
                pltpu.SMEM((units,), F32),
                pltpu.SMEM((units,), F32),
                pltpu.SMEM((1, 1), jnp.int32),
                pltpu.VMEM((SLOTS, CASES), BF16),
                pltpu.VMEM((units, 1, SLOTS), F32),
                pltpu.VMEM((1, SLOTS), F32),
                pltpu.VMEM((1, SLOTS), jnp.int32),
                pltpu.VMEM((SLOTS, SLOTS), BF16),
                pltpu.VMEM((SLOTS, CORNERS), BF16),
                pltpu.VMEM((CORNERS, CORNERS), F32),
                pltpu.VMEM((SLOTS, SLOTS), BF16),
                pltpu.VMEM((SLOTS, SLOTS), BF16),
                pltpu.VMEM((2 * CORNERS, SLOTS), BF16),
                pltpu.VMEM((SLOTS, 2 * CORNERS), BF16),
                pltpu.VMEM((SLOTS, 3 * CORNERS), BF16),
                pltpu.VMEM((5 * CORNERS, CASES), BF16),
                pltpu.VMEM((SLOTS, 2 * CASES), BF16),
                pltpu.VMEM((2, SLOTS, CASES), BF16),
                pltpu.VMEM((SLOTS, CASES), F32),
                pltpu.VMEM((3, 3, OWN, CASES), CONTRIB),
                pltpu.VMEM((3, 6, OWN, CASES), CONTRIB),
                pltpu.VMEM((2, CORNERS, CASES), F32),
                pltpu.VMEM((CORNERS, CASES), F32),
                pltpu.VMEM((2, HALF, CASES), F32),
                pltpu.VMEM((2, HALF + SUMS, CASES), BF16),
                pltpu.VMEM((2, chips - 1, HALF + SUMS, CASES), BF16),
                pltpu.VMEM((2, HALF + SUMS, CASES), F32),
                pltpu.VMEM((2, HALF + SUMS, CASES), F32),
                pltpu.VMEM((spans, 4, CASES), F32),
                dma((10,)),
                dma((3, 6)),
                dma((3, 6)),
                dma((6,)),
                dma((6,)),
                dma((8,)),
                dma((2,)),
                dma((2, 2)),
                dma((2, 2)),
                dma((2, 2)),
                dma((2,)),
            ],
            compiler_params=pltpu.CompilerParams(
                collective_id=0, has_side_effects=True, vmem_limit_bytes=60 * 2**20
            ),
        )(
            retard,
            compliance,
            lengths.reshape(1, 1),
            stress,
            history,
            micro,
            multiplier_index,
            dual_block,
            corner_map,
            coarse_stiffness_inverse,
        )
        return first * v0 - second * v1, v0 - first * v1 + second * v2

    rows = P(("span", "sub"), None)
    blocks = P(("span", "sub"), None, None)
    return jax.shard_map(
        on_device,
        mesh=mesh,
        in_specs=(
            blocks,
            P(None, ("span", "sub"), None),
            P(),
            P(),
            rows,
            P(("span", "sub")),
            rows,
            blocks,
            blocks,
            P("span", None, None),
        ),
        out_specs=(rows, rows),
        check_vma=False,
    )
```

```python
import functools

import jax
import jax.numpy as jnp
from jax import lax
from jax.experimental import pallas as pl
from jax.experimental.pallas import tpu as pltpu
from jax.sharding import PartitionSpec as P

MESH = pl.DeviceIdType.MESH
F32 = jnp.float32
BF16 = jnp.bfloat16
CONTRIB = jnp.bfloat16
OWN = 256
SLOTS = 768
CASES = 128
CORNERS = 128
HALF = CORNERS // 2
SUMS = 16
ROWS = 64


def dot(a, b):
    return jnp.dot(a, b, preferred_element_type=F32)


def two_parts(x):
    high = x.astype(BF16)
    return high, (x - high.astype(F32)).astype(BF16)


def column_sum(x):
    return jnp.sum(x, axis=0, keepdims=True)


def as_column(row):
    return jnp.transpose(jnp.broadcast_to(row, (CASES, SLOTS)))


def sum_rows(values):
    row = lax.broadcasted_iota(jnp.int32, (SUMS, CASES), 0)
    out = jnp.zeros((SUMS, CASES), F32)
    for number, value in enumerate(values):
        base, rest = 3 * number, value
        for i in range(3):
            part = rest.astype(BF16).astype(F32)
            rest = rest - part
            out = jnp.where(row == base + i, part, out)
    return out


def kernel(
    spans,
    subs,
    retard_hbm,
    compliance_hbm,
    lengths_hbm,
    stress_hbm,
    history_hbm,
    micro_hbm,
    index_hbm,
    dual_hbm,
    corner_hbm,
    stiff_hbm,
    basis0,
    basis1,
    basis2,
    factor0,
    factor1,
    retard,
    compliance,
    lengths,
    stress,
    history,
    micro,
    index,
    dual,
    corner,
    stiff,
    pick,
    pick_t,
    corner_t,
    corner_w,
    coarse,
    w_near,
    split,
    window,
    local_window,
    contrib_out,
    contrib_in,
    w_part,
    w_full,
    chip_in,
    ring_out,
    ring_in,
    pair_out,
    pair_in,
    totals,
    load_sem,
    contrib_send,
    contrib_recv,
    coarse_send,
    coarse_recv,
    near_send,
    near_recv,
    chip_sem,
    ring_sem,
    pair_sem,
    total_sem,
):
    basis = (basis0, basis1, basis2)
    p = lax.axis_index("span")
    s = lax.axis_index("sub")
    chips = subs // 2
    core = lax.rem(s, 2)
    partner = (p, s + 1 - 2 * core)
    mine = pl.ds(pl.multiple_of(core * HALF, HALF), HALF)
    theirs = pl.ds(pl.multiple_of((1 - core) * HALF, HALF), HALF)

    loads = [
        pltpu.make_async_copy(src, dst, load_sem.at[i])
        for i, (src, dst) in enumerate(
            (
                (lengths_hbm, lengths),
                (index_hbm, index),
                (retard_hbm, retard),
                (compliance_hbm, compliance),
                (micro_hbm, micro),
                (history_hbm, history),
                (stress_hbm.at[0], stress),
                (corner_hbm.at[0], corner),
                (dual_hbm.at[0], dual),
                (stiff_hbm.at[0], stiff),
            )
        )
    ]
    for copy in loads:
        copy.start()

    barrier = pltpu.get_barrier_semaphore()

    def greet_span(d, carry):
        pl.semaphore_signal(
            barrier, inc=1, device_id=(lax.rem(p + d, spans), s), device_id_type=MESH
        )
        return carry

    def greet_chip(d, carry):
        pl.semaphore_signal(
            barrier, inc=1, device_id=(p, lax.rem(s + 2 * d, subs)), device_id_type=MESH
        )
        return carry

    pl.semaphore_signal(barrier, inc=1, device_id=partner, device_id_type=MESH)
    for d in (1, spans - 1, 2, spans - 2):
        greet_span(d, 0)
        pl.semaphore_signal(
            barrier, inc=1, device_id=(lax.rem(p + d, spans), partner[1]), device_id_type=MESH
        )
    lax.fori_loop(1, chips, greet_chip, 0)
    lax.fori_loop(3, spans - 2, greet_span, 0)

    loads[0].wait()
    loads[1].wait()
    slot = lax.broadcasted_iota(jnp.int32, (1, SLOTS), 1)
    owner_span = index[...] // (OWN * subs)
    place = (owner_span - p + 1) * OWN + lax.rem(index[...], OWN)
    place = jnp.where(slot < lengths[0, 0], place, -1)

    def build_pick(i, carry):
        rows = pl.ds(pl.multiple_of(i * ROWS, ROWS), ROWS)
        at = lax.broadcasted_iota(jnp.int32, (ROWS, SLOTS), 0) + i * ROWS
        pick[rows, :] = jnp.where(at == place, 1.0, 0.0).astype(BF16)
        return carry

    lax.fori_loop(0, SLOTS // ROWS, build_pick, 0)

    for copy in loads[2:6]:
        copy.wait()
    creep = jnp.zeros((1, SLOTS), F32)
    past = jnp.zeros((1, SLOTS), F32)
    for k in range(history.shape[0]):
        weight = 1.0 - jnp.exp(-1.0 / jnp.full((1, SLOTS), retard[k], F32))
        creep = creep + weight * compliance[k]
        past = past + weight * history[k]
    relaxed = micro[...] / (1.0 + micro[...])
    scale = as_column(creep + 0.5 * relaxed)
    past = as_column(past)
    loads[6].wait()
    load = scale * stress[...].astype(F32) - past
    high, low = two_parts(load)
    split[:, :CASES] = high
    split[:, CASES:] = low

    def picked(rows):
        both = dot(pick[rows, :], split[...])
        return both[:, :CASES] + both[:, CASES:]

    routes = ((1, 1), (2, 2), (2, 1), (0, -1), (1, -1), (0, -2))

    def contrib_copy(k, i):
        block, onward = routes[i]
        return pltpu.make_async_remote_copy(
            src_ref=contrib_out.at[k, block],
            dst_ref=contrib_in.at[k, i],
            send_sem=contrib_send.at[k, i],
            recv_sem=contrib_recv.at[k, i],
            device_id=(lax.rem(p + spans + onward, spans), s),
            device_id_type=MESH,
        )

    landing = ((0, 1), (0, 0), (1, 0), (1, 2), (2, 1), (2, 2))

    def coarse_copy(i):
        block, onward = routes[i]
        row, column = landing[i]
        return pltpu.make_async_remote_copy(
            src_ref=coarse.at[pl.ds(block * OWN, OWN), pl.ds((2 - block) * CORNERS, CORNERS)],
            dst_ref=coarse.at[pl.ds(row * OWN, OWN), pl.ds(column * CORNERS, CORNERS)],
            send_sem=coarse_send.at[i],
            recv_sem=coarse_recv.at[i],
            device_id=(lax.rem(p + spans + onward, spans), s),
            device_id_type=MESH,
        )

    def near_copies():
        kept = w_near.at[pl.ds(pl.multiple_of(2 * CORNERS + core * HALF, HALF), HALF)]
        copies = []
        for onward in (2, -2, 1, -1):
            place = pl.multiple_of((2 - onward) * CORNERS + core * HALF, HALF)
            for to in (s, partner[1]):
                copies.append(
                    pltpu.make_async_remote_copy(
                        src_ref=kept,
                        dst_ref=w_near.at[pl.ds(place, HALF)],
                        send_sem=near_send.at[len(copies)],
                        recv_sem=near_recv.at[0 if onward > 0 else 1],
                        device_id=(lax.rem(p + spans + onward, spans), to),
                        device_id_type=MESH,
                    )
                )
        return copies

    def all_near(side):
        rows = w_near.at[pl.ds(side * 3 * CORNERS, 2 * CORNERS)]
        return pltpu.make_async_remote_copy(
            src_ref=rows,
            dst_ref=rows,
            send_sem=near_send.at[0],
            recv_sem=near_recv.at[side],
            device_id=partner,
            device_id_type=MESH,
        )

    def used_routes(k):
        return range(6) if k < 2 else (2, 3)

    def chip_copy(k):
        return pltpu.make_async_remote_copy(
            src_ref=w_part.at[k, theirs],
            dst_ref=chip_in.at[k],
            send_sem=chip_sem.at[k, 0],
            recv_sem=chip_sem.at[k, 1],
            device_id=partner,
            device_id_type=MESH,
        )

    ring_rows = (HALF, HALF + SUMS)

    def ring_part(part):
        return pl.ds(part * HALF, SUMS if part else HALF)

    def ring_copies(k, part):
        return [
            pltpu.make_async_remote_copy(
                src_ref=ring_out.at[k, ring_part(part)],
                dst_ref=ring_in.at[k, d - 1, ring_part(part)],
                send_sem=ring_sem.at[k + part, 0],
                recv_sem=ring_sem.at[k + part, 1],
                device_id=(p, lax.rem(s + 2 * d, subs)),
                device_id_type=MESH,
            )
            for d in sorted(range(1, chips), key=lambda d: -min(d, chips - d))
        ]

    def all_ring(k, part):
        return pltpu.make_async_remote_copy(
            src_ref=ring_in.at[k, :, ring_part(part)],
            dst_ref=ring_in.at[k, :, ring_part(part)],
            send_sem=ring_sem.at[k + part, 0],
            recv_sem=ring_sem.at[k + part, 1],
            device_id=partner,
            device_id_type=MESH,
        )

    def pair_copy(k):
        return pltpu.make_async_remote_copy(
            src_ref=pair_out.at[k, pl.ds(0, ring_rows[k])],
            dst_ref=pair_in.at[k, pl.ds(0, ring_rows[k])],
            send_sem=pair_sem.at[k, 0],
            recv_sem=pair_sem.at[k, 1],
            device_id=partner,
            device_id_type=MESH,
        )

    def send_totals():
        def step(i, carry):
            d = 1 + lax.rem(i + spans // 3, spans - 1)
            pltpu.make_async_remote_copy(
                src_ref=totals.at[0],
                dst_ref=totals.at[d],
                send_sem=total_sem.at[0],
                recv_sem=total_sem.at[1],
                device_id=(lax.rem(p + d, spans), s),
                device_id_type=MESH,
            ).start()
            return carry

        lax.fori_loop(0, spans - 1, step, 0)

    def all_totals():
        rest = totals.at[pl.ds(1, spans - 1)]
        return pltpu.make_async_remote_copy(
            src_ref=rest,
            dst_ref=rest,
            send_sem=total_sem.at[0],
            recv_sem=total_sem.at[1],
            device_id=partner,
            device_id_type=MESH,
        )

    previous, own, following = blocks = [slice(i * OWN, (i + 1) * OWN) for i in range(3)]

    def send_contribs(k, image):
        for block in (0, 2, 1) if k < 2 else (0, 2):
            value = image(blocks[block])
            if k < 2:
                local_window[blocks[block], :] = value
            contrib_out[k, block] = value.astype(CONTRIB)
            if k == 0 and block == 0:
                pl.semaphore_wait(barrier, spans + chips + 3)
            for i in sorted(used_routes(k), key=lambda i: -abs(routes[i][1])):
                if routes[i][0] == block:
                    contrib_copy(k, i).start()

    def receive_contribs(k):
        for i in used_routes(k):
            contrib_copy(k, i).wait_recv()

        def arrived(i):
            return contrib_in[k, i].astype(F32)

        if k == 1:
            for i in used_routes(k):
                coarse_copy(i).wait_recv()
            for side in range(2):
                all_near(side).wait_recv()
            for block in range(3):
                near = w_near[block * CORNERS : (block + 3) * CORNERS, :]
                local_window[blocks[block], :] += dot(coarse[blocks[block], :], near)
        basis[k][...] = local_window[own, :] + arrived(2) + arrived(3)
        if k < 2:
            window[k, previous] = (local_window[previous, :] + arrived(0) + arrived(1)).astype(BF16)
            window[k, own] = basis[k][...].astype(BF16)
            window[k, following] = (local_window[following, :] + arrived(4) + arrived(5)).astype(
                BF16
            )

    send_contribs(0, picked)

    loads[7].wait()
    reach = dot(pick[...], corner[...])
    loads[9].wait()
    spread = jnp.dot(reach, stiff[...], precision=lax.Precision.HIGHEST, preferred_element_type=F32)
    for block in range(3):
        coarse[blocks[block], (2 - block) * CORNERS : (3 - block) * CORNERS] = spread[
            blocks[block]
        ].astype(BF16)

    high, low = two_parts(reach)
    corner_w[:, :CORNERS] = high
    corner_w[:, CORNERS:] = low
    high, low = two_parts(jnp.transpose(reach))
    corner_t[:CORNERS, :] = high
    corner_t[CORNERS:, :] = low
    place_t = as_column(place.astype(F32))

    def build_pick_t(j, carry):
        lanes = pl.ds(pl.multiple_of(j * CASES, CASES), CASES)
        at = lax.broadcasted_iota(jnp.int32, (SLOTS, CASES), 1) + j * CASES
        pick_t[:, lanes] = jnp.where(place_t == at.astype(F32), 1.0, 0.0).astype(BF16)
        return carry

    lax.fori_loop(0, SLOTS // CASES, build_pick_t, 0)
    loads[8].wait()
    for i in used_routes(0):
        contrib_copy(0, i).wait_send()
    for i in reversed(used_routes(0)):
        coarse_copy(i).start()
    receive_contribs(0)
    products_so_far, energies = [], []
    for k in range(2):
        both = dot(corner_t[...], window[k])
        w_part[k] = both[:CORNERS] + both[CORNERS:]
        chip_copy(k).start()
        u = dot(pick_t[...], window[k]).astype(BF16)

        def products():
            products_so_far.append(column_sum(basis[k][...] * basis[k][...]))
            y = dot(dual[...], u)
            products_so_far.append(column_sum(u.astype(F32) * y))
            return y

        chip_copy(k).wait_recv()
        half = w_part[k, mine] + chip_in[k]
        ring_out[k, :HALF] = half.astype(BF16)
        for copy in ring_copies(k, 0):
            copy.start()
        y = products()
        if k == 1:
            ring_sums = sum_rows(products_so_far)
            ring_out[k, HALF:] = ring_sums.astype(BF16)
            for copy in ring_copies(k, 1):
                copy.start()
        high, low = two_parts(y)
        split[:, :CASES] = high
        split[:, CASES:] = low
        if k == 0:
            send_contribs(1, picked)
        else:
            for block in blocks:
                local_window[block, :] = picked(block)
        for part in range(k + 1):
            all_ring(k, part).wait_recv()
        for d in range(chips - 1):
            half = half + ring_in[k, d, :HALF].astype(F32)
            if k == 1:
                ring_sums = ring_sums + ring_in[k, d, HALF:].astype(F32)
        pair_out[k, :HALF] = half
        if k == 1:
            pair_out[k, HALF:] = ring_sums
        pair_copy(k).start()
        if k == 0:
            w_near[pl.ds(pl.multiple_of(2 * CORNERS + core * HALF, HALF), HALF), :] = half.astype(
                BF16
            )
            for copy in near_copies():
                copy.start()
        w_full[mine, :] = half
        pair_copy(k).wait_recv()
        w_full[theirs, :] = pair_in[k, :HALF]
        if k == 0:
            w_near[pl.ds(pl.multiple_of(3 * CORNERS - HALF - core * HALF, HALF), HALF), :] = pair_in[
                k, :HALF
            ].astype(BF16)
        w = w_full[...]
        z = jnp.dot(stiff[...], w, precision=lax.Precision.HIGHEST, preferred_element_type=F32)
        z_narrow = z.astype(BF16)
        z_twice = jnp.concatenate([z_narrow, z_narrow], axis=0)

        def image(rows):
            return local_window[rows, :] + dot(corner_w[rows, :], z_twice)

        energies.append(column_sum(w * z_narrow.astype(F32)))
        if k == 1:
            ring_sums = ring_sums + pair_in[k, HALF:]
            for i in range(4):
                row = column_sum(ring_sums[3 * i : 3 * i + 3])
                totals[0, i : i + 1] = row + energies[i // 2] if i % 2 else row
            send_totals()
            send_contribs(2, image)
        if k == 1:
            local_window[own, :] = image(own)
        receive_contribs(k + 1)

    all_totals().wait_recv()
    products = jnp.sum(totals[...], axis=0)
    g00, g01, g11, g12 = (products[i : i + 1] for i in range(4))
    alpha0 = g00 / g01
    norm1 = g00 - 2.0 * alpha0 * g01 + alpha0 * alpha0 * g11
    beta = norm1 / g00
    grown = 1.0 + beta
    curve = grown * grown * g01 - 2.0 * grown * alpha0 * g11 + alpha0 * alpha0 * g12
    alpha1 = norm1 / curve
    factor0[...] = alpha0 + alpha1 * grown
    factor1[...] = alpha0 * alpha1
    all_totals().wait_send()

    tail = near_copies() + [coarse_copy(i) for i in range(6)]
    for k in range(1, 3):
        for i in used_routes(k):
            contrib_copy(k, i).wait_send()
    for k in range(2):
        for copy in [chip_copy(k), pair_copy(k)] + [all_ring(k, i) for i in range(k + 1)] + (tail if k == 0 else []):
            copy.wait_send()


def solution(mesh):
    spans, subs = mesh.shape["span"], mesh.shape["sub"]
    chips = subs // 2
    vmem = pl.BlockSpec(memory_space=pltpu.VMEM)
    hbm = pl.BlockSpec(memory_space=pl.ANY)
    dma = pltpu.SemaphoreType.DMA

    def on_device(
        stress,
        history,
        retard,
        compliance,
        micro,
        lengths,
        multiplier_index,
        dual_block,
        corner_map,
        coarse_stiffness_inverse,
    ):
        units = history.shape[0]
        v0, v1, v2, first, second = pl.pallas_call(
            functools.partial(kernel, spans, subs),
            name="creep_step",
            out_shape=[pltpu.VMEM((OWN, CASES), F32)] * 3
            + [pltpu.VMEM((1, CASES), F32)] * 2,
            in_specs=[hbm] * 10,
            out_specs=[vmem] * 5,
            scratch_shapes=[
                pltpu.SMEM((units,), F32),
                pltpu.SMEM((units,), F32),
                pltpu.SMEM((1, 1), jnp.int32),
                pltpu.VMEM((SLOTS, CASES), BF16),
                pltpu.VMEM((units, 1, SLOTS), F32),
                pltpu.VMEM((1, SLOTS), F32),
                pltpu.VMEM((1, SLOTS), jnp.int32),
                pltpu.VMEM((SLOTS, SLOTS), BF16),
                pltpu.VMEM((SLOTS, CORNERS), BF16),
                pltpu.VMEM((CORNERS, CORNERS), F32),
                pltpu.VMEM((SLOTS, SLOTS), BF16),
                pltpu.VMEM((SLOTS, SLOTS), BF16),
                pltpu.VMEM((2 * CORNERS, SLOTS), BF16),
                pltpu.VMEM((SLOTS, 2 * CORNERS), BF16),
                pltpu.VMEM((SLOTS, 3 * CORNERS), BF16),
                pltpu.VMEM((5 * CORNERS, CASES), BF16),
                pltpu.VMEM((SLOTS, 2 * CASES), BF16),
                pltpu.VMEM((2, SLOTS, CASES), BF16),
                pltpu.VMEM((SLOTS, CASES), F32),
                pltpu.VMEM((3, 3, OWN, CASES), CONTRIB),
                pltpu.VMEM((3, 6, OWN, CASES), CONTRIB),
                pltpu.VMEM((2, CORNERS, CASES), F32),
                pltpu.VMEM((CORNERS, CASES), F32),
                pltpu.VMEM((2, HALF, CASES), F32),
                pltpu.VMEM((2, HALF + SUMS, CASES), BF16),
                pltpu.VMEM((2, chips - 1, HALF + SUMS, CASES), BF16),
                pltpu.VMEM((2, HALF + SUMS, CASES), F32),
                pltpu.VMEM((2, HALF + SUMS, CASES), F32),
                pltpu.VMEM((spans, 4, CASES), F32),
                dma((10,)),
                dma((3, 6)),
                dma((3, 6)),
                dma((6,)),
                dma((6,)),
                dma((8,)),
                dma((2,)),
                dma((2, 2)),
                dma((3, 2)),
                dma((2, 2)),
                dma((2,)),
            ],
            compiler_params=pltpu.CompilerParams(
                collective_id=0, has_side_effects=True, vmem_limit_bytes=60 * 2**20
            ),
        )(
            retard,
            compliance,
            lengths.reshape(1, 1),
            stress,
            history,
            micro,
            multiplier_index,
            dual_block,
            corner_map,
            coarse_stiffness_inverse,
        )
        return first * v0 - second * v1, v0 - first * v1 + second * v2

    rows = P(("span", "sub"), None)
    blocks = P(("span", "sub"), None, None)
    return jax.shard_map(
        on_device,
        mesh=mesh,
        in_specs=(
            blocks,
            P(None, ("span", "sub"), None),
            P(),
            P(),
            rows,
            P(("span", "sub")),
            rows,
            blocks,
            blocks,
            P("span", None, None),
        ),
        out_specs=(rows, rows),
        check_vma=False,
    )
```

```python
import functools

import jax
import jax.numpy as jnp
from jax import lax
from jax.experimental import pallas as pl
from jax.experimental.pallas import tpu as pltpu
from jax.sharding import PartitionSpec as P

MESH = pl.DeviceIdType.MESH
F32 = jnp.float32
BF16 = jnp.bfloat16
CONTRIB = jnp.bfloat16
OWN = 256
SLOTS = 768
CASES = 128
CORNERS = 128
HALF = CORNERS // 2
SUMS = 16
ROWS = 64


def dot(a, b):
    return jnp.dot(a, b, preferred_element_type=F32)


def two_parts(x):
    high = x.astype(BF16)
    return high, (x - high.astype(F32)).astype(BF16)


def column_sum(x):
    return jnp.sum(x, axis=0, keepdims=True)


def as_column(row):
    return jnp.transpose(jnp.broadcast_to(row, (CASES, SLOTS)))


def sum_rows(values):
    row = lax.broadcasted_iota(jnp.int32, (SUMS, CASES), 0)
    out = jnp.zeros((SUMS, CASES), F32)
    for number, value in enumerate(values):
        base, rest = 3 * number, value
        for i in range(3):
            part = rest.astype(BF16).astype(F32)
            rest = rest - part
            out = jnp.where(row == base + i, part, out)
    return out


def kernel(
    spans,
    subs,
    retard_hbm,
    compliance_hbm,
    lengths_hbm,
    stress_hbm,
    history_hbm,
    micro_hbm,
    index_hbm,
    dual_hbm,
    corner_hbm,
    stiff_hbm,
    basis0,
    basis1,
    basis2,
    factor0,
    factor1,
    retard,
    compliance,
    lengths,
    stress,
    history,
    micro,
    index,
    dual,
    corner,
    stiff,
    pick,
    pick_t,
    corner_t,
    corner_w,
    coarse,
    w_near,
    split,
    window,
    local_window,
    contrib_out,
    contrib_in,
    w_part,
    w_full,
    chip_in,
    ring_out,
    ring_in,
    pair_out,
    pair_in,
    totals,
    load_sem,
    contrib_send,
    contrib_recv,
    coarse_send,
    coarse_recv,
    near_send,
    near_recv,
    chip_sem,
    ring_sem,
    pair_sem,
    total_sem,
):
    basis = (basis0, basis1, basis2)
    p = lax.axis_index("span")
    s = lax.axis_index("sub")
    chips = subs // 2
    core = lax.rem(s, 2)
    partner = (p, s + 1 - 2 * core)
    mine = pl.ds(pl.multiple_of(core * HALF, HALF), HALF)
    theirs = pl.ds(pl.multiple_of((1 - core) * HALF, HALF), HALF)

    loads = [
        pltpu.make_async_copy(src, dst, load_sem.at[i])
        for i, (src, dst) in enumerate(
            (
                (lengths_hbm, lengths),
                (index_hbm, index),
                (retard_hbm, retard),
                (compliance_hbm, compliance),
                (micro_hbm, micro),
                (history_hbm, history),
                (stress_hbm.at[0], stress),
                (corner_hbm.at[0], corner),
                (dual_hbm.at[0], dual),
                (stiff_hbm.at[0], stiff),
            )
        )
    ]
    for copy in loads:
        copy.start()

    barrier = pltpu.get_barrier_semaphore()

    def greet_span(d, carry):
        pl.semaphore_signal(
            barrier, inc=1, device_id=(lax.rem(p + d, spans), s), device_id_type=MESH
        )
        return carry

    def greet_chip(d, carry):
        pl.semaphore_signal(
            barrier, inc=1, device_id=(p, lax.rem(s + 2 * d, subs)), device_id_type=MESH
        )
        return carry

    pl.semaphore_signal(barrier, inc=1, device_id=partner, device_id_type=MESH)
    for d in (1, spans - 1, 2, spans - 2):
        greet_span(d, 0)
        pl.semaphore_signal(
            barrier, inc=1, device_id=(lax.rem(p + d, spans), partner[1]), device_id_type=MESH
        )
    lax.fori_loop(1, chips, greet_chip, 0)
    lax.fori_loop(3, spans - 2, greet_span, 0)

    loads[0].wait()
    loads[1].wait()
    slot = lax.broadcasted_iota(jnp.int32, (1, SLOTS), 1)
    owner_span = index[...] // (OWN * subs)
    place = (owner_span - p + 1) * OWN + lax.rem(index[...], OWN)
    place = jnp.where(slot < lengths[0, 0], place, -1)

    def build_pick(i, carry):
        rows = pl.ds(pl.multiple_of(i * ROWS, ROWS), ROWS)
        at = lax.broadcasted_iota(jnp.int32, (ROWS, SLOTS), 0) + i * ROWS
        pick[rows, :] = jnp.where(at == place, 1.0, 0.0).astype(BF16)
        return carry

    lax.fori_loop(0, SLOTS // ROWS, build_pick, 0)

    for copy in loads[2:6]:
        copy.wait()
    creep = jnp.zeros((1, SLOTS), F32)
    past = jnp.zeros((1, SLOTS), F32)
    for k in range(history.shape[0]):
        weight = 1.0 - jnp.exp(-1.0 / jnp.full((1, SLOTS), retard[k], F32))
        creep = creep + weight * compliance[k]
        past = past + weight * history[k]
    relaxed = micro[...] / (1.0 + micro[...])
    scale = as_column(creep + 0.5 * relaxed)
    past = as_column(past)
    loads[6].wait()
    load = scale * stress[...].astype(F32) - past
    high, low = two_parts(load)
    split[:, :CASES] = high
    split[:, CASES:] = low

    def picked(rows):
        both = dot(pick[rows, :], split[...])
        return both[:, :CASES] + both[:, CASES:]

    routes = ((1, 1), (2, 2), (2, 1), (0, -1), (1, -1), (0, -2))

    def contrib_copy(k, i):
        block, onward = routes[i]
        return pltpu.make_async_remote_copy(
            src_ref=contrib_out.at[k, block],
            dst_ref=contrib_in.at[k, i],
            send_sem=contrib_send.at[k, i],
            recv_sem=contrib_recv.at[k, i],
            device_id=(lax.rem(p + spans + onward, spans), s),
            device_id_type=MESH,
        )

    landing = ((0, 1), (0, 0), (1, 0), (1, 2), (2, 1), (2, 2))

    def coarse_copy(i):
        block, onward = routes[i]
        row, column = landing[i]
        return pltpu.make_async_remote_copy(
            src_ref=coarse.at[pl.ds(block * OWN, OWN), pl.ds((2 - block) * CORNERS, CORNERS)],
            dst_ref=coarse.at[pl.ds(row * OWN, OWN), pl.ds(column * CORNERS, CORNERS)],
            send_sem=coarse_send.at[i],
            recv_sem=coarse_recv.at[i],
            device_id=(lax.rem(p + spans + onward, spans), s),
            device_id_type=MESH,
        )

    def near_copies():
        kept = w_near.at[pl.ds(pl.multiple_of(2 * CORNERS + core * HALF, HALF), HALF)]
        copies = []
        for onward in (2, -2, 1, -1):
            place = pl.multiple_of((2 - onward) * CORNERS + core * HALF, HALF)
            for to in (s, partner[1]):
                copies.append(
                    pltpu.make_async_remote_copy(
                        src_ref=kept,
                        dst_ref=w_near.at[pl.ds(place, HALF)],
                        send_sem=near_send.at[len(copies)],
                        recv_sem=near_recv.at[0 if onward > 0 else 1],
                        device_id=(lax.rem(p + spans + onward, spans), to),
                        device_id_type=MESH,
                    )
                )
        return copies

    def all_near(side):
        rows = w_near.at[pl.ds(side * 3 * CORNERS, 2 * CORNERS)]
        return pltpu.make_async_remote_copy(
            src_ref=rows,
            dst_ref=rows,
            send_sem=near_send.at[0],
            recv_sem=near_recv.at[side],
            device_id=partner,
            device_id_type=MESH,
        )

    def used_routes(k):
        return range(6) if k < 2 else (2, 3)

    def chip_copy(k):
        return pltpu.make_async_remote_copy(
            src_ref=w_part.at[k, theirs],
            dst_ref=chip_in.at[k],
            send_sem=chip_sem.at[k, 0],
            recv_sem=chip_sem.at[k, 1],
            device_id=partner,
            device_id_type=MESH,
        )

    ring_rows = (HALF, HALF + SUMS)

    def ring_copies(k):
        return [
            pltpu.make_async_remote_copy(
                src_ref=ring_out.at[k, pl.ds(0, ring_rows[k])],
                dst_ref=ring_in.at[k, d - 1, pl.ds(0, ring_rows[k])],
                send_sem=ring_sem.at[k, 0],
                recv_sem=ring_sem.at[k, 1],
                device_id=(p, lax.rem(s + 2 * d, subs)),
                device_id_type=MESH,
            )
            for d in sorted(range(1, chips), key=lambda d: -min(d, chips - d))
        ]

    def all_ring(k):
        return pltpu.make_async_remote_copy(
            src_ref=ring_in.at[k, :, pl.ds(0, ring_rows[k])],
            dst_ref=ring_in.at[k, :, pl.ds(0, ring_rows[k])],
            send_sem=ring_sem.at[k, 0],
            recv_sem=ring_sem.at[k, 1],
            device_id=partner,
            device_id_type=MESH,
        )

    def pair_copy(k):
        return pltpu.make_async_remote_copy(
            src_ref=pair_out.at[k, pl.ds(0, ring_rows[k])],
            dst_ref=pair_in.at[k, pl.ds(0, ring_rows[k])],
            send_sem=pair_sem.at[k, 0],
            recv_sem=pair_sem.at[k, 1],
            device_id=partner,
            device_id_type=MESH,
        )

    def send_totals():
        def step(i):
            d = 1 + (i + spans // 3) % (spans - 1)
            pltpu.make_async_remote_copy(
                src_ref=totals.at[0],
                dst_ref=totals.at[d],
                send_sem=total_sem.at[0],
                recv_sem=total_sem.at[1],
                device_id=(lax.rem(p + d, spans), s),
                device_id_type=MESH,
            ).start()

        for i in range(spans - 1):
            step(i)

    def all_totals():
        rest = totals.at[pl.ds(1, spans - 1)]
        return pltpu.make_async_remote_copy(
            src_ref=rest,
            dst_ref=rest,
            send_sem=total_sem.at[0],
            recv_sem=total_sem.at[1],
            device_id=partner,
            device_id_type=MESH,
        )

    previous, own, following = blocks = [slice(i * OWN, (i + 1) * OWN) for i in range(3)]

    def send_contribs(k, image):
        for block in (0, 2, 1) if k < 2 else (0, 2):
            value = image(blocks[block])
            if k < 2:
                local_window[blocks[block], :] = value
            contrib_out[k, block] = value.astype(CONTRIB)
            if k == 0 and block == 0:
                pl.semaphore_wait(barrier, spans + chips + 3)
            for i in sorted(used_routes(k), key=lambda i: -abs(routes[i][1])):
                if routes[i][0] == block:
                    contrib_copy(k, i).start()

    def receive_contribs(k):
        for i in used_routes(k):
            contrib_copy(k, i).wait_recv()

        def arrived(i):
            return contrib_in[k, i].astype(F32)

        if k == 1:
            for i in used_routes(k):
                coarse_copy(i).wait_recv()
            for side in range(2):
                all_near(side).wait_recv()
            for block in range(3):
                near = w_near[block * CORNERS : (block + 3) * CORNERS, :]
                local_window[blocks[block], :] += dot(coarse[blocks[block], :], near)
        basis[k][...] = local_window[own, :] + arrived(2) + arrived(3)
        if k < 2:
            window[k, previous] = (local_window[previous, :] + arrived(0) + arrived(1)).astype(BF16)
            window[k, own] = basis[k][...].astype(BF16)
            window[k, following] = (local_window[following, :] + arrived(4) + arrived(5)).astype(
                BF16
            )

    send_contribs(0, picked)

    loads[7].wait()
    reach = dot(pick[...], corner[...])
    loads[9].wait()
    spread = jnp.dot(reach, stiff[...], precision=lax.Precision.HIGHEST, preferred_element_type=F32)
    for block in range(3):
        coarse[blocks[block], (2 - block) * CORNERS : (3 - block) * CORNERS] = spread[
            blocks[block]
        ].astype(BF16)

    high, low = two_parts(reach)
    corner_w[:, :CORNERS] = high
    corner_w[:, CORNERS:] = low
    high, low = two_parts(jnp.transpose(reach))
    corner_t[:CORNERS, :] = high
    corner_t[CORNERS:, :] = low
    place_t = as_column(place.astype(F32))

    def build_pick_t(j, carry):
        lanes = pl.ds(pl.multiple_of(j * CASES, CASES), CASES)
        at = lax.broadcasted_iota(jnp.int32, (SLOTS, CASES), 1) + j * CASES
        pick_t[:, lanes] = jnp.where(place_t == at.astype(F32), 1.0, 0.0).astype(BF16)
        return carry

    lax.fori_loop(0, SLOTS // CASES, build_pick_t, 0)
    loads[8].wait()
    for i in used_routes(0):
        contrib_copy(0, i).wait_send()
    for i in reversed(used_routes(0)):
        coarse_copy(i).start()
    receive_contribs(0)
    products_so_far, energies = [], []
    for k in range(2):
        both = dot(corner_t[...], window[k])
        w_part[k] = both[:CORNERS] + both[CORNERS:]
        chip_copy(k).start()
        u = dot(pick_t[...], window[k]).astype(BF16)

        def products():
            products_so_far.append(column_sum(basis[k][...] * basis[k][...]))
            y = dot(dual[...], u)
            products_so_far.append(column_sum(u.astype(F32) * y))
            return y

        if k == 1:
            y = products()
            ring_sums = sum_rows(products_so_far)
            ring_out[k, HALF:] = ring_sums.astype(BF16)
        chip_copy(k).wait_recv()
        half = w_part[k, mine] + chip_in[k]
        ring_out[k, :HALF] = half.astype(BF16)
        for copy in ring_copies(k):
            copy.start()
        if k == 0:
            y = products()
        high, low = two_parts(y)
        split[:, :CASES] = high
        split[:, CASES:] = low
        if k == 0:
            send_contribs(1, picked)
        else:
            for block in blocks:
                local_window[block, :] = picked(block)
        all_ring(k).wait_recv()
        for d in range(chips - 1):
            half = half + ring_in[k, d, :HALF].astype(F32)
            if k == 1:
                ring_sums = ring_sums + ring_in[k, d, HALF:].astype(F32)
        pair_out[k, :HALF] = half
        if k == 1:
            pair_out[k, HALF:] = ring_sums
        pair_copy(k).start()
        if k == 0:
            w_near[pl.ds(pl.multiple_of(2 * CORNERS + core * HALF, HALF), HALF), :] = half.astype(
                BF16
            )
            for copy in near_copies():
                copy.start()
        w_full[mine, :] = half
        pair_copy(k).wait_recv()
        w_full[theirs, :] = pair_in[k, :HALF]
        if k == 0:
            w_near[pl.ds(pl.multiple_of(3 * CORNERS - HALF - core * HALF, HALF), HALF), :] = pair_in[
                k, :HALF
            ].astype(BF16)
        w = w_full[...]
        z = jnp.dot(stiff[...], w, precision=lax.Precision.HIGHEST, preferred_element_type=F32)
        z_narrow = z.astype(BF16)
        z_twice = jnp.concatenate([z_narrow, z_narrow], axis=0)

        def image(rows):
            return local_window[rows, :] + dot(corner_w[rows, :], z_twice)

        energies.append(column_sum(w * z_narrow.astype(F32)))
        if k == 1:
            ring_sums = ring_sums + pair_in[k, HALF:]
            for i in range(4):
                row = column_sum(ring_sums[3 * i : 3 * i + 3])
                totals[0, i : i + 1] = row + energies[i // 2] if i % 2 else row
            send_totals()
            send_contribs(2, image)
        if k == 1:
            local_window[own, :] = image(own)
        receive_contribs(k + 1)

    all_totals().wait_recv()
    products = jnp.sum(totals[...], axis=0)
    g00, g01, g11, g12 = (products[i : i + 1] for i in range(4))
    alpha0 = g00 / g01
    norm1 = g00 - 2.0 * alpha0 * g01 + alpha0 * alpha0 * g11
    beta = norm1 / g00
    grown = 1.0 + beta
    curve = grown * grown * g01 - 2.0 * grown * alpha0 * g11 + alpha0 * alpha0 * g12
    alpha1 = norm1 / curve
    factor0[...] = alpha0 + alpha1 * grown
    factor1[...] = alpha0 * alpha1
    all_totals().wait_send()

    tail = near_copies() + [coarse_copy(i) for i in range(6)]
    for k in range(1, 3):
        for i in used_routes(k):
            contrib_copy(k, i).wait_send()
    for k in range(2):
        for copy in [chip_copy(k), pair_copy(k), all_ring(k)] + (tail if k == 0 else []):
            copy.wait_send()


def solution(mesh):
    spans, subs = mesh.shape["span"], mesh.shape["sub"]
    chips = subs // 2
    vmem = pl.BlockSpec(memory_space=pltpu.VMEM)
    hbm = pl.BlockSpec(memory_space=pl.ANY)
    dma = pltpu.SemaphoreType.DMA

    def on_device(
        stress,
        history,
        retard,
        compliance,
        micro,
        lengths,
        multiplier_index,
        dual_block,
        corner_map,
        coarse_stiffness_inverse,
    ):
        units = history.shape[0]
        v0, v1, v2, first, second = pl.pallas_call(
            functools.partial(kernel, spans, subs),
            name="creep_step",
            out_shape=[pltpu.VMEM((OWN, CASES), F32)] * 3
            + [pltpu.VMEM((1, CASES), F32)] * 2,
            in_specs=[hbm] * 10,
            out_specs=[vmem] * 5,
            scratch_shapes=[
                pltpu.SMEM((units,), F32),
                pltpu.SMEM((units,), F32),
                pltpu.SMEM((1, 1), jnp.int32),
                pltpu.VMEM((SLOTS, CASES), BF16),
                pltpu.VMEM((units, 1, SLOTS), F32),
                pltpu.VMEM((1, SLOTS), F32),
                pltpu.VMEM((1, SLOTS), jnp.int32),
                pltpu.VMEM((SLOTS, SLOTS), BF16),
                pltpu.VMEM((SLOTS, CORNERS), BF16),
                pltpu.VMEM((CORNERS, CORNERS), F32),
                pltpu.VMEM((SLOTS, SLOTS), BF16),
                pltpu.VMEM((SLOTS, SLOTS), BF16),
                pltpu.VMEM((2 * CORNERS, SLOTS), BF16),
                pltpu.VMEM((SLOTS, 2 * CORNERS), BF16),
                pltpu.VMEM((SLOTS, 3 * CORNERS), BF16),
                pltpu.VMEM((5 * CORNERS, CASES), BF16),
                pltpu.VMEM((SLOTS, 2 * CASES), BF16),
                pltpu.VMEM((2, SLOTS, CASES), BF16),
                pltpu.VMEM((SLOTS, CASES), F32),
                pltpu.VMEM((3, 3, OWN, CASES), CONTRIB),
                pltpu.VMEM((3, 6, OWN, CASES), CONTRIB),
                pltpu.VMEM((2, CORNERS, CASES), F32),
                pltpu.VMEM((CORNERS, CASES), F32),
                pltpu.VMEM((2, HALF, CASES), F32),
                pltpu.VMEM((2, HALF + SUMS, CASES), BF16),
                pltpu.VMEM((2, chips - 1, HALF + SUMS, CASES), BF16),
                pltpu.VMEM((2, HALF + SUMS, CASES), F32),
                pltpu.VMEM((2, HALF + SUMS, CASES), F32),
                pltpu.VMEM((spans, 4, CASES), F32),
                dma((10,)),
                dma((3, 6)),
                dma((3, 6)),
                dma((6,)),
                dma((6,)),
                dma((8,)),
                dma((2,)),
                dma((2, 2)),
                dma((2, 2)),
                dma((2, 2)),
                dma((2,)),
            ],
            compiler_params=pltpu.CompilerParams(
                collective_id=0, has_side_effects=True, vmem_limit_bytes=60 * 2**20
            ),
        )(
            retard,
            compliance,
            lengths.reshape(1, 1),
            stress,
            history,
            micro,
            multiplier_index,
            dual_block,
            corner_map,
            coarse_stiffness_inverse,
        )
        return first * v0 - second * v1, v0 - first * v1 + second * v2

    rows = P(("span", "sub"), None)
    blocks = P(("span", "sub"), None, None)
    return jax.shard_map(
        on_device,
        mesh=mesh,
        in_specs=(
            blocks,
            P(None, ("span", "sub"), None),
            P(),
            P(),
            rows,
            P(("span", "sub")),
            rows,
            blocks,
            blocks,
            P("span", None, None),
        ),
        out_specs=(rows, rows),
        check_vma=False,
    )
```
